32 devices in a mesh: seq: 16 (over z, y, x), tp: 2 (over core).
Axes of the slice: x: 2, y: 2, z: 4, core: 2. Of those that a mesh axis runs over, the one named last changes fastest.
Arguments:
- x_proj: bfloat16 [8192, 8192], P('seq', 'tp'), may hold values from -27 to 27
- bc_proj: bfloat16 [8192, 2, 1024], P('seq', None, 'tp'), may hold values from -6 to 6
- z_proj: bfloat16 [8192, 8192], P('seq', 'tp'), may hold values from -6 to 6
- dt_raw: float32 [8192, 128], P('seq', 'tp'), may hold values from -2.5 to 63
- conv_x: bfloat16 [4, 8192], P(None, 'tp'), may hold values from -3 to 3
- conv_bc: bfloat16 [4, 2, 1024], P(None, None, 'tp'), may hold values from -3 to 3
- bias_x: float32 [8192], P('tp'), may hold values from -0.5 to 0.5
- bias_bc: float32 [2, 1024], P(None, 'tp'), may hold values from -0.5 to 0.5
- dt_bias: float32 [128], P('tp'), may hold values from -4.5 to -3
- a_log: float32 [128], P('tp'), may hold values from -5.5 to 0.5
- d_skip: float32 [128], P('tp'), may hold values from 0.15 to 5
- norm_gain: float32 [8192], P('tp'), may hold values from 0.1 to 1.9
- seg_ids: int32 [8192], P('seq'), may hold values from 0 to 15, never falling along the last dimension, each value on 1 to 2048 neighbouring positions
Outputs:
- normed: bfloat16 [8192, 8192], P('seq', 'tp')
The draws below stay inside these ranges and needn't reach their ends.
Inputs may be any that keep to these rules, and one draw needn't show every extreme that they name: `seg_ids`: each prompt's tokens are contiguous; ids start at 0 and never fall, each id from 0 to 15 has one token or more, at most 2048 tokens, and one prompt has exactly 2048.
All inputs are finite; a program needn't handle non-finite values.
Results may differ from the reference program's by a relative error of at most 0.0036.
Values may be sent and summed in bfloat16 or wider, within the bound.
A program may use at most 128 MiB of HBM per device.

```python
import math
import jax
import jax.numpy as jnp
import numpy as np
from jax import lax

HEADS = 128
HEAD_DIM = 64
GROUPS = 8
STATE = 128
CONV_K = 4
STRETCH = 256
TOK_DEV = 512
REQS = 16
INNER = 8192
PACKED_TOKENS = 8192
MOST = 2048


def draw_x_proj(key, part):
    row_key, col_key, value_key = jax.random.split(key, 3)
    row_scale = jnp.exp(jax.random.uniform(row_key, (PACKED_TOKENS, 1)) * math.log(10.0)) * 0.3
    col_scale = jnp.exp(jax.random.uniform(col_key, (1, INNER)) * math.log(10.0)) * 0.3
    values = jnp.clip(jax.random.normal(value_key, (PACKED_TOKENS, INNER)), -3.0, 3.0) * row_scale * col_scale
    return values.astype(jnp.bfloat16)


def draw_dt_raw(key, part):
    jitter_random_key, block_random_key, spike_random_key = jax.random.split(key, 3)
    random_jitter = jnp.clip(jax.random.normal(jitter_random_key, (PACKED_TOKENS, HEADS)) * 0.5, -1.5, 1.5)
    block_shift = jax.random.uniform(block_random_key, (PACKED_TOKENS // TOK_DEV, HEADS), minval=-0.7, maxval=0.7)
    moved_values = jnp.repeat(block_shift, TOK_DEV, axis=0)
    chosen_positions = jax.random.randint(spike_random_key, (8,), 0, PACKED_TOKENS)
    spike_values = jnp.any(jnp.arange(PACKED_TOKENS)[:, None] == chosen_positions[None, :], axis=1).astype(jnp.float32)
    return (random_jitter + moved_values + 60.0 * spike_values[:, None]).astype(jnp.float32)


def draw_a_log(key, part):
    kind_key, slow_key, fast_key = jax.random.split(key, 3)
    slow = jax.random.uniform(slow_key, (HEADS,), minval=-5.5, maxval=-4.8)
    chosen = jax.random.bernoulli(kind_key, 0.5, (HEADS,))
    fast = jax.random.uniform(fast_key, (HEADS,), minval=-2.0, maxval=0.5)
    return jnp.where(chosen, slow, fast).astype(jnp.float32)


def draw_d_skip(key, part):
    order = jnp.arange(HEADS, dtype=jnp.float32) / HEADS
    base = jnp.exp(math.log(0.3) + math.log(10.0) * order)
    factor = jax.random.uniform(key, (HEADS,), minval=0.8, maxval=1.25)
    return (base * factor).astype(jnp.float32)


def steps_of(own_key, extent, shards, least, top_value):
    def one(position, shards_of):
        steps = jax.random.uniform(jax.random.fold_in(jax.random.fold_in(own_key, 6), position), (shards_of,), jnp.float32, least / len(shards), top_value / len(shards))
        return jnp.repeat(jnp.exp(steps), extent[position] // shards_of).reshape((-1,) + (1,) * (len(extent) - position - 1))

    gain = one(*shards[0])
    for cut in shards[1:]:
        gain = gain * one(*cut)
    return gain


def length_profile(amount, total, most, lean):
    portions = [(1 << 20) // math.isqrt(rank ** lean) + 1 for rank in range(2, amount + 1)]
    surplus, given = total - most - (amount - 1), [1] * (amount - 1)
    while surplus > 0:
        candidates = [i for i in range(amount - 1) if given[i] < most]
        mass, remaining = sum([portions[i] for i in candidates]), surplus
        for i in candidates:
            addition = min(most - given[i], max(1, remaining * portions[i] // mass), surplus)
            given[i] = given[i] + addition
            surplus = surplus - addition
    return np.array([most] + given)


def uneven_parts(stream_key, count, total, limit, slope):
    if count == 2:
        one = jax.random.randint(stream_key, (), max(1, total - limit), min(limit, total - 1) + 1)
        return jnp.stack([one, total - one])
    lengths = jnp.asarray(length_profile(count, total, limit, slope), jnp.int32)
    twos = (count - 1) // 2
    donor, receiver = lengths[1:1 + 2 * twos:2], lengths[2:2 + 2 * twos:2]
    room = jnp.minimum(donor - 1, limit - receiver)
    passed = jax.random.randint(jax.random.fold_in(stream_key, 1), (twos,), 0, 1 << 20) % (room + 1)
    lengths = lengths.at[1:1 + 2 * twos:2].set(donor - passed).at[2:2 + 2 * twos:2].set(receiver + passed)
    return lengths[jax.random.permutation(jax.random.fold_in(stream_key, 2), count)]


def gaussian(own_key, dims, deviation, reach, cuts=(), kind=jnp.bfloat16):
    drawn = jax.random.normal(own_key, dims, jnp.float32) * deviation
    if len(cuts) > 0:
        drawn = steps_of(own_key, dims, cuts, -0.22, 0.18) * drawn
    return jnp.clip(drawn, min=-reach, max=reach).astype(kind)


def setup_inputs(seed: int = 0) -> dict:
    key_of = jax.random.split(jax.random.key(seed), 14)
    return {
        "x_proj": draw_x_proj(jax.random.fold_in(key_of[13], 71), 0),
        "bc_proj": gaussian(key_of[1], (PACKED_TOKENS, 2, GROUPS * STATE), 1.0, 6.0, ((0, 16), (2, 2))),
        "z_proj": gaussian(key_of[2], (PACKED_TOKENS, INNER), 1.0, 6.0, ((0, 16), (1, 2))),
        "dt_raw": draw_dt_raw(jax.random.fold_in(key_of[13], 71), 0),
        "conv_x": gaussian(key_of[4], (CONV_K, INNER), CONV_K ** -0.5, 3.0, ((1, 2),)),
        "conv_bc": gaussian(key_of[5], (CONV_K, 2, GROUPS * STATE), CONV_K ** -0.5, 3.0, ((2, 2),)),
        "bias_x": jnp.clip(jax.random.uniform(key_of[6], (INNER,), jnp.float32, -0.5, 0.5) * steps_of(key_of[6], (INNER,), ((0, 2),), -0.4, 0.0), -0.5, 0.5),
        "bias_bc": jnp.clip(jax.random.uniform(key_of[7], (2, GROUPS * STATE), jnp.float32, -0.5, 0.5) * steps_of(key_of[7], (2, GROUPS * STATE), ((1, 2),), -0.4, 0.0), -0.5, 0.5),
        "dt_bias": jnp.clip(-4.5 + 1.5 * jax.random.uniform(key_of[8], (HEADS,), jnp.float32) ** steps_of(key_of[8], (HEADS,), ((0, 2),), -0.2, 0.2), -4.5, -3.0),
        "a_log": draw_a_log(jax.random.fold_in(key_of[13], 71), 0),
        "d_skip": draw_d_skip(jax.random.fold_in(key_of[13], 71), 0),
        "norm_gain": jnp.clip(1.0 + 0.18 * jax.random.normal(key_of[11], (INNER,), jnp.float32), 0.1, 1.9),
        "seg_ids": jnp.searchsorted(jnp.cumsum(uneven_parts(key_of[12], REQS, PACKED_TOKENS, MOST, 2)), jnp.arange(PACKED_TOKENS), side="right").astype(jnp.int32),
    }


def causal_conv(window, window_ids, weight, bias, rows):
    taps = weight.shape[0]
    own_ids = window_ids[taps - 1:]
    extra = (1,) * (window.ndim - 1)
    result = jnp.broadcast_to(bias.astype(jnp.float32), (rows,) + bias.shape)
    for offset in range(taps):
        piece = window[offset:offset + rows].astype(jnp.float32)
        same = (window_ids[offset:offset + rows] == own_ids).reshape((rows,) + extra)
        result = result + jnp.where(same, piece * weight[offset].astype(jnp.float32), 0.0)
    return jax.nn.silu(result).astype(jnp.bfloat16)

def reference(x_proj, bc_proj, z_proj, dt_raw, conv_x, conv_bc, bias_x, bias_bc, dt_bias, a_log, d_skip, norm_gain, seg_ids):
    heads_group = HEADS // GROUPS
    margin = CONV_K - 1
    token_ids = seg_ids.astype(jnp.float32)
    x_pad = jnp.concatenate([jnp.zeros((margin, INNER), jnp.bfloat16), x_proj])
    bc_pad = jnp.concatenate([jnp.zeros((margin, 2, GROUPS * STATE), jnp.bfloat16), bc_proj])
    id_pad = jnp.concatenate([jnp.zeros((margin,), jnp.float32), token_ids])
    rate = -jnp.exp(a_log)
    lower = jnp.tril(jnp.ones((STRETCH, STRETCH), dtype=bool))
    skip = d_skip.reshape(GROUPS, heads_group)[..., None]

    def advance(state, index):
        begin = (index * STRETCH).astype(jnp.int32)
        x_window = lax.dynamic_slice_in_dim(x_pad, begin, STRETCH + margin, 0)
        bc_window = lax.dynamic_slice_in_dim(bc_pad, begin, STRETCH + margin, 0)
        id_window = lax.dynamic_slice_in_dim(id_pad, begin, STRETCH + margin, 0)
        own = id_window[margin:]
        before = id_window[margin - 1]
        x_conv = causal_conv(x_window, id_window, conv_x, bias_x, STRETCH)
        bc_conv = causal_conv(bc_window, id_window, conv_bc, bias_bc, STRETCH)
        step_size = jax.nn.softplus(lax.dynamic_slice_in_dim(dt_raw, begin, STRETCH, 0) + dt_bias)
        cumul = jnp.cumsum(step_size * rate, axis=0)
        cum_heads = cumul.T.reshape(GROUPS, heads_group, STRETCH)
        step_heads = step_size.T.reshape(GROUPS, heads_group, STRETCH)
        b_in = bc_conv[:, 0].reshape(STRETCH, GROUPS, STATE).astype(jnp.float32)
        c_out = bc_conv[:, 1].reshape(STRETCH, GROUPS, STATE).astype(jnp.float32)
        same = (own[:, None] == own[None, :]) & lower
        scores = jnp.einsum('qgn,sgn->gqs', c_out, b_in)
        spread = cum_heads[..., :, None] - cum_heads[..., None, :]
        decay = jnp.where(same, jnp.exp(jnp.where(same, spread, 0.0)), 0.0)
        mixing = (scores[:, None] * decay * step_heads[:, :, None, :]).astype(jnp.bfloat16)
        x_heads = x_conv.reshape(STRETCH, GROUPS, heads_group, HEAD_DIM).astype(jnp.float32)
        y_intra = jnp.einsum('ghqs,sghp->qghp', mixing.astype(jnp.float32), x_heads)
        tail_same = (own == own[-1]).astype(jnp.float32)
        weights = jnp.exp(cum_heads[..., -1:] - cum_heads) * step_heads * tail_same
        b_weighted = (jnp.transpose(b_in, (1, 0, 2))[:, None] * weights[..., None]).astype(jnp.bfloat16)
        increment = jnp.einsum('ghsn,sghp->ghpn', b_weighted.astype(jnp.float32), x_heads)
        carry_gain = jnp.exp(cum_heads[..., -1]) * (own[-1] == before).astype(jnp.float32)
        link = jnp.exp(cum_heads) * (own == before).astype(jnp.float32)
        y_inter = jnp.einsum('qgn,ghpn->qghp', c_out, state, precision=lax.Precision.HIGHEST) * jnp.transpose(link, (2, 0, 1))[..., None]
        new_state = carry_gain[..., None, None] * state + increment
        mixed = y_intra + y_inter + skip * x_heads
        z_block = lax.dynamic_slice_in_dim(z_proj, begin, STRETCH, 0).astype(jnp.float32)
        gated = mixed.reshape(STRETCH, INNER) * jax.nn.silu(z_block)
        scale = lax.rsqrt(lax.optimization_barrier(jnp.sum(gated * gated, axis=-1)) / INNER + 1e-05)
        return (new_state, (gated * scale[:, None] * norm_gain).astype(jnp.bfloat16))
    start_state = jnp.zeros((GROUPS, heads_group, HEAD_DIM, STATE), jnp.float32)
    _, outputs = lax.scan(advance, start_state, jnp.arange(PACKED_TOKENS // STRETCH, dtype=jnp.int32))
    return outputs.reshape(PACKED_TOKENS, INNER)
```

```python
import jax
import jax.numpy as jnp
from jax import lax
from jax.experimental import pallas as pl
from jax.experimental.pallas import tpu as pltpu
from jax.sharding import PartitionSpec as P

STATE = 128
STRETCH = 256
RIM = 8
LOG2E = 1.4426950408889634
F32 = jnp.float32
BF16 = jnp.bfloat16
VMEM = 52 * 1024 * 1024


def silu(v):
    half = 0.5 * v
    return half * jnp.tanh(half) + half


def conv_tile(window, weight, bias, masks, start, rows, lanes):
    acc = jnp.broadcast_to(bias, (rows, lanes.stop - lanes.start))
    for tap in range(4):
        piece = window[pl.ds(RIM - 3 + tap + start, rows), lanes]
        term = piece * weight[tap : tap + 1]
        if tap < 3:
            term = term * masks[tap, pl.ds(start, rows), :]
        acc = acc + term
    return silu(acc).astype(BF16)


def local_kernel(
    x_ref, rim_ref, b_ref, c_ref, rimb_ref, rimc_ref, wx_ref, wb_ref, wc_ref,
    bx_ref, bb_ref, bc_ref, masks, tail_ref, gain_ref, row_gain_ref, expand_ref,
    xo_ref, bo_ref, co_ref, inc_ref, sum_ref, window, window_b, window_c, weighted,
):
    rows, width = x_ref.shape
    blocks = rows // STRETCH
    window[0:RIM] = rim_ref[...].astype(F32)
    window_b[0:RIM] = rimb_ref[...].astype(F32)
    window_c[0:RIM] = rimc_ref[...].astype(F32)
    window_b[RIM:] = b_ref[...].astype(F32)
    window_c[RIM:] = c_ref[...].astype(F32)
    one = slice(0, STATE)
    for block in range(blocks):
        at = slice(block * STRETCH, (block + 1) * STRETCH)
        bo_ref[at] = conv_tile(
            window_b, wb_ref[...].astype(F32), bb_ref[...], masks, at.start, STRETCH, one
        )
        co_ref[at] = conv_tile(
            window_c, wc_ref[...].astype(F32), bc_ref[...], masks, at.start, STRETCH, one
        )
    for tile in range(width // 128):
        lanes = slice(tile * 128, (tile + 1) * 128)
        window[RIM:, lanes] = x_ref[:, lanes].astype(F32)
        weight = wx_ref[:, lanes].astype(F32)
        for block in range(blocks):
            at = slice(block * STRETCH, (block + 1) * STRETCH)
            value = conv_tile(window, weight, bx_ref[:, lanes], masks, at.start, STRETCH, lanes)
            xo_ref[at, lanes] = value
            spread = jnp.dot(
                tail_ref[0, at, :], expand_ref[:, lanes], preferred_element_type=F32
            )
            weighted[at, lanes] = (value.astype(F32) * spread).astype(BF16)
    parts = []
    for block in range(blocks):
        at = slice(block * STRETCH, (block + 1) * STRETCH)
        parts.append(
            lax.dot_general(
                bo_ref[at], weighted[at], (((0,), (0,)), ((), ())), preferred_element_type=F32
            )
        )
    inc_ref[0] = parts[0]
    sum_ref[0, 0:STATE] = (row_gain_ref[1:2] * parts[0] + parts[1]).astype(BF16)
    sum_ref[0, STATE:] = gain_ref[0]


def intra_kernel(
    x_ref, b_ref, c_ref, col_ref, row_ref, ids_ref, idr_ref, skip_ref, y_ref
):
    rows, width = x_ref.shape
    blocks = rows // STRETCH
    half = STRETCH // 2
    lane = lax.broadcasted_iota(jnp.int32, (STRETCH, 128), 1)
    first = lane < 64
    t_at = lax.broadcasted_iota(jnp.int32, (STRETCH, STRETCH), 0)
    s_at = lax.broadcasted_iota(jnp.int32, (STRETCH, STRETCH), 1)
    lower = s_at <= t_at
    for block in range(blocks):
        at = slice(block * STRETCH, (block + 1) * STRETCH)
        scores = lax.dot_general(
            c_ref[at], b_ref[at], (((1,), (1,)), ((), ())), preferred_element_type=F32
        )
        same = (ids_ref[at] == idr_ref[block : block + 1]) & lower
        scores = jnp.where(same, scores, 0.0)
        top, left, right = scores[:half, :half], scores[half:, :half], scores[half:, half:]
        for pair in range(width // 128):
            lanes = slice(pair * 128, (pair + 1) * 128)
            value = x_ref[at, lanes]
            upper_sum = lower_sum = None
            for which in range(2):
                head = 2 * pair + which
                keep = first if which == 0 else jnp.logical_not(first)
                mine = jnp.where(keep, value.astype(F32), 0.0).astype(BF16)
                col = col_ref[0, at, head : head + 1]
                row = row_ref[0, block, head : head + 1, :]
                m_top = top * jnp.exp2(jnp.minimum(col[:half] - row[:, :half], 80.0))
                m_left = left * jnp.exp2(col[half:] - row[:, :half])
                m_right = right * jnp.exp2(jnp.minimum(col[half:] - row[:, half:], 80.0))
                m_low = jnp.concatenate([m_left.astype(BF16), m_right.astype(BF16)], axis=1)
                up = jnp.dot(m_top.astype(BF16), mine[:half], preferred_element_type=F32)
                low = jnp.dot(m_low, mine, preferred_element_type=F32)
                upper_sum = up if which == 0 else upper_sum + up
                lower_sum = low if which == 0 else lower_sum + low
            skip = skip_ref[:, lanes]
            wide = value.astype(F32)
            y_ref[at.start : at.start + half, lanes] = upper_sum + skip * wide[:half]
            y_ref[at.start + half : at.stop, lanes] = lower_sum + skip * wide[half:]


def gate_kernel(
    y_ref, z_ref, c_ref, link_ref, expand_ref, enter_ref, inc_ref, row_gain_ref, out_ref, sq_ref
):
    rows, width = y_ref.shape
    blocks = rows // STRETCH

    @pl.when(pl.program_id(0) == 0)
    def _():
        sq_ref[...] = jnp.zeros_like(sq_ref)

    for tile in range(width // 256):
        lanes = slice(tile * 256, (tile + 1) * 256)
        state = enter_ref[0, :, lanes]
        for block in range(blocks):
            at = slice(block * STRETCH, (block + 1) * STRETCH)
            if block == 1:
                state = (
                    row_gain_ref[0:1, lanes] * state.astype(F32) + inc_ref[0, :, lanes]
                ).astype(BF16)
            inter = jnp.dot(c_ref[at], state, preferred_element_type=F32)
            link = jnp.dot(link_ref[0, at], expand_ref[:, lanes], preferred_element_type=F32)
            gate = silu(z_ref[at, lanes].astype(F32))
            gated = (y_ref[at, lanes] + inter * link) * gate
            out_ref[at, lanes] = gated
            square = gated * gated
            sq_ref[at] += square[:, :128] + square[:, 128:]


def split_two(value):
    high = value.astype(BF16)
    return jnp.concatenate([high, (value - high.astype(F32)).astype(BF16)], axis=-1)


def exchange(sums, groups):
    axis = "seq"
    count = lax.axis_size(axis)
    plane = count // 4
    mine = lax.axis_index(axis)
    place = mine % plane
    _, depth, width = sums.shape
    cut = groups * width // plane
    split = plane // groups
    chunks = sums.reshape(groups, depth, split, cut).transpose(0, 2, 1, 3)
    chunks = chunks.reshape(plane, depth, cut)

    def pick(array, index):
        return lax.dynamic_index_in_dim(array, index, 0, keepdims=False)

    def swap(array):
        got = [pick(array, place)]
        for k in range(1, plane):
            got.append(
                lax.ppermute(pick(array, place ^ k), axis, [(i, i ^ k) for i in range(count)])
            )
        return jnp.stack(got)

    came = swap(chunks)
    run = jnp.zeros((STATE, cut), F32)
    through = jnp.ones((1, cut), F32)
    entering, gains = [], []
    for source in range(plane):
        part = pick(came, place ^ source)
        gain = part[STATE : STATE + 1].astype(F32) + part[STATE + 1 : STATE + 2].astype(F32)
        entering.append(run)
        gains.append(through)
        run = gain * run + part[:STATE].astype(F32)
        through = through * gain
    before = lax.ppermute(
        run.astype(BF16), axis, [(i, i + plane) for i in range(count - plane)]
    ).astype(F32)
    ready = jnp.stack([(e + g * before).astype(BF16) for e, g in zip(entering, gains)])
    back = swap(ready)
    final = jnp.stack([pick(back, place ^ owner) for owner in range(plane)])
    final = final.reshape(groups, split, STATE, cut).transpose(0, 2, 1, 3)
    return final.reshape(groups, STATE, width)


def on_device(
    x_proj, bc_proj, z_proj, dt_raw, conv_x, conv_bc, bias_x, bias_bc, dt_bias, a_log,
    d_skip, norm_gain, seg_ids,
):
    rows, inner = x_proj.shape
    heads = dt_raw.shape[1]
    groups = bc_proj.shape[2] // STATE
    per = heads // groups
    size = inner // heads
    width = inner // groups
    blocks = rows // STRETCH
    seq = lax.axis_size("seq")
    bc_flat = bc_proj.reshape(rows, 2 * groups * STATE)
    wbc = conv_bc.reshape(4, 2 * groups * STATE)
    bbc = bias_bc.reshape(1, 2 * groups * STATE)
    route = [(i, i + 1) for i in range(seq - 1)]
    rim_x = lax.ppermute(x_proj[rows - RIM :], "seq", route)
    rim_bc = lax.ppermute(bc_flat[rows - RIM :], "seq", route)
    rim_ids = lax.ppermute(seg_ids[rows - RIM :], "seq", route)
    window_ids = jnp.concatenate([rim_ids, seg_ids])
    masks = jnp.stack(
        [(window_ids[RIM - 3 + k : RIM - 3 + k + rows] == seg_ids).astype(F32) for k in range(3)]
    )
    masks = jnp.broadcast_to(masks[:, :, None], (3, rows, 128))

    step = jax.nn.softplus(dt_raw + dt_bias)
    rate = -jnp.exp(a_log) * LOG2E
    tri = jnp.tril(jnp.ones((STRETCH, STRETCH), F32))
    logs = (step * rate).reshape(blocks, STRETCH, heads)
    cum = jnp.einsum("ts,csh->cth", tri, logs, precision=lax.Precision.HIGHEST)
    last = cum[:, -1:]
    ids = seg_ids.reshape(blocks, STRETCH)
    before = window_ids[RIM - 1 : RIM - 1 + rows : STRETCH]
    steps = step.reshape(blocks, STRETCH, heads)
    tail = jnp.exp2(last - cum) * steps * (ids == ids[:, -1:]).astype(F32)[..., None]
    link = jnp.exp2(cum) * (ids == before[:, None]).astype(F32)[..., None]
    gain = jnp.exp2(last[:, 0]) * (ids[:, -1] == before).astype(F32)[:, None]

    def by_group(value):
        return value.reshape(rows, groups, per).transpose(1, 0, 2)

    tail_two = split_two(by_group(tail))
    link_two = split_two(by_group(link))
    col = by_group(cum)
    shifted = cum - jnp.log2(steps)
    row = shifted.reshape(blocks, STRETCH, groups, per).transpose(2, 0, 3, 1)
    row_gain = jnp.repeat(gain, size, axis=1)
    whole = row_gain[0] * row_gain[1]
    whole_high = whole.astype(BF16)
    whole_low = (whole - whole_high.astype(F32)).astype(BF16)
    gain_rows = jnp.stack([whole_high, whole_low]).reshape(2, groups, width).transpose(1, 0, 2)
    gain_rows = jnp.pad(gain_rows, ((0, 0), (0, 14), (0, 0)))
    expand = (
        lax.broadcasted_iota(jnp.int32, (2 * per, width), 0) % per
        == lax.broadcasted_iota(jnp.int32, (2 * per, width), 1) // size
    ).astype(BF16)

    params = pltpu.CompilerParams(vmem_limit_bytes=VMEM)
    wide = lambda n: pl.BlockSpec((n, width), lambda g: (0, g))
    state_b = lambda n: pl.BlockSpec((n, STATE), lambda g: (0, g))
    state_c = lambda n: pl.BlockSpec((n, STATE), lambda g: (0, g + groups))
    lead = lambda *shape: pl.BlockSpec((1,) + shape, lambda g: (g,) + (0,) * len(shape))
    full = lambda *shape: pl.BlockSpec(shape, lambda g: (0,) * len(shape))
    bias_row = bias_x.reshape(1, inner)
    x_conv, b_conv, c_conv, inc, sums = pl.pallas_call(
        local_kernel,
        grid=(groups,),
        in_specs=[
            wide(rows), wide(RIM), state_b(rows), state_c(rows), state_b(RIM), state_c(RIM),
            wide(4), state_b(4), state_c(4), wide(1), state_b(1), state_c(1),
            full(3, rows, 128), lead(rows, 2 * per), lead(16, width), wide(blocks),
            full(2 * per, width),
        ],
        out_specs=[
            wide(rows), state_b(rows), state_b(rows), lead(STATE, width),
            lead(STATE + 16, width),
        ],
        out_shape=[
            jax.ShapeDtypeStruct((rows, inner), BF16),
            jax.ShapeDtypeStruct((rows, groups * STATE), BF16),
            jax.ShapeDtypeStruct((rows, groups * STATE), BF16),
            jax.ShapeDtypeStruct((groups, STATE, width), F32),
            jax.ShapeDtypeStruct((groups, STATE + 16, width), BF16),
        ],
        scratch_shapes=[
            pltpu.VMEM((rows + RIM, width), F32),
            pltpu.VMEM((rows + RIM, STATE), F32),
            pltpu.VMEM((rows + RIM, STATE), F32),
            pltpu.VMEM((rows, width), BF16),
        ],
        compiler_params=params,
        cost_estimate=pl.CostEstimate(
            flops=4 * rows * inner * STATE, bytes_accessed=30 << 20, transcendentals=rows * inner
        ),
        name="local",
    )(
        x_proj, rim_x, bc_flat, bc_flat, rim_bc, rim_bc, conv_x, wbc, wbc, bias_row, bbc, bbc,
        masks, tail_two, gain_rows, row_gain, expand,
    )

    enter = exchange(sums, groups)

    y = pl.pallas_call(
        intra_kernel,
        grid=(groups,),
        in_specs=[
            wide(rows), state_b(rows), state_b(rows), lead(rows, per),
            lead(blocks, per, STRETCH), full(rows, 1), full(blocks, STRETCH), wide(1),
        ],
        out_specs=wide(rows),
        out_shape=jax.ShapeDtypeStruct((rows, inner), F32),
        compiler_params=params,
        cost_estimate=pl.CostEstimate(
            flops=40 * rows * inner * STRETCH, bytes_accessed=100 << 20,
            transcendentals=rows * heads * STRETCH,
        ),
        name="intra",
    )(
        x_conv, b_conv, c_conv, col, row, seg_ids.reshape(rows, 1), ids,
        jnp.repeat(d_skip, size).reshape(1, inner),
    )

    gated, squares = pl.pallas_call(
        gate_kernel,
        grid=(groups,),
        in_specs=[
            wide(rows), wide(rows), state_b(rows), lead(rows, 2 * per), full(2 * per, width),
            lead(STATE, width), lead(STATE, width), wide(blocks),
        ],
        out_specs=[wide(rows), full(rows, 128)],
        out_shape=[
            jax.ShapeDtypeStruct((rows, inner), F32),
            jax.ShapeDtypeStruct((rows, 128), F32),
        ],
        compiler_params=params,
        name="gate",
    )(y, z_proj, c_conv, link_two, expand, enter, inc, row_gain)

    total = jnp.sum(squares, axis=-1)
    count = lax.axis_size("tp")
    own = total
    for k in range(1, count):
        total = total + lax.ppermute(own, "tp", [(i, (i + k) % count) for i in range(count)])
    scale = lax.rsqrt(total / (inner * count) + 1e-05)
    return (gated * scale[:, None] * norm_gain).astype(BF16)


def solution(mesh):
    in_specs = (
        P("seq", "tp"),
        P("seq", None, "tp"),
        P("seq", "tp"),
        P("seq", "tp"),
        P(None, "tp"),
        P(None, None, "tp"),
        P("tp"),
        P(None, "tp"),
        P("tp"),
        P("tp"),
        P("tp"),
        P("tp"),
        P("seq"),
    )
    return jax.shard_map(
        on_device, mesh=mesh, in_specs=in_specs, out_specs=P("seq", "tp"), check_vma=False
    )
```

```python
import functools

import jax
import jax.numpy as jnp
from jax import lax
from jax.experimental import pallas as pl
from jax.experimental.pallas import tpu as pltpu
from jax.sharding import PartitionSpec as P

STATE = 128
STRETCH = 256
RIM = 8
LOG2E = 1.4426950408889634
F32 = jnp.float32
BF16 = jnp.bfloat16
VMEM = 52 * 1024 * 1024


def silu(v):
    half = 0.5 * v
    return half * jnp.tanh(half) + half


def conv_tile(window, weight, bias, masks, start, rows):
    acc = jnp.broadcast_to(bias, (rows, 128))
    for tap in range(4):
        piece = window[pl.ds(RIM - 3 + tap + start, rows), :]
        term = piece * weight[tap : tap + 1]
        if tap < 3:
            term = term * masks[tap, pl.ds(start, rows), :]
        acc = acc + term
    return silu(acc).astype(BF16)


def local_kernel(
    x_ref, rim_ref, b_ref, c_ref, rimb_ref, rimc_ref, wx_ref, wb_ref, wc_ref,
    bx_ref, bb_ref, bc_ref, counted_ref, tail_ref, gain_ref, row_gain_ref, expand_ref,
    xo_ref, bo_ref, co_ref, inc_ref, sum_ref, window, window_b, window_c, weighted, masks,
):
    rows, width = x_ref.shape
    blocks = rows // STRETCH

    @pl.when(pl.program_id(0) == 0)
    def _():
        for tap in range(3):
            masks[tap] = jnp.broadcast_to(counted_ref[:, tap : tap + 1], (rows, 128))

    window_b[0:RIM] = rimb_ref[...].astype(F32)
    window_c[0:RIM] = rimc_ref[...].astype(F32)
    window_b[RIM:] = b_ref[...].astype(F32)
    window_c[RIM:] = c_ref[...].astype(F32)
    for block in range(blocks):
        at = slice(block * STRETCH, (block + 1) * STRETCH)
        bo_ref[at] = conv_tile(
            window_b, wb_ref[...].astype(F32), bb_ref[...], masks, at.start, STRETCH
        )
        co_ref[at] = conv_tile(
            window_c, wc_ref[...].astype(F32), bc_ref[...], masks, at.start, STRETCH
        )
    for tile in range(width // 128):
        lanes = slice(tile * 128, (tile + 1) * 128)
        window[tile, 0:RIM] = rim_ref[:, lanes].astype(F32)
        window[tile, RIM:] = x_ref[:, lanes].astype(F32)
        weight = wx_ref[:, lanes].astype(F32)
        for block in range(blocks):
            at = slice(block * STRETCH, (block + 1) * STRETCH)
            value = conv_tile(
                window.at[tile], weight, bx_ref[:, lanes], masks, at.start, STRETCH
            )
            xo_ref[at, lanes] = value
            spread = jnp.dot(
                tail_ref[0, at, :], expand_ref[:, lanes], preferred_element_type=F32
            )
            weighted[at, lanes] = (value.astype(F32) * spread).astype(BF16)
    parts = []
    for block in range(blocks):
        at = slice(block * STRETCH, (block + 1) * STRETCH)
        parts.append(
            lax.dot_general(
                bo_ref[at], weighted[at], (((0,), (0,)), ((), ())), preferred_element_type=F32
            )
        )
    inc_ref[0] = parts[0]
    sum_ref[0, 0:STATE] = (row_gain_ref[1:2] * parts[0] + parts[1]).astype(BF16)
    sum_ref[0, STATE:] = gain_ref[0]


def intra_kernel(
    x_ref, b_ref, c_ref, col_ref, row_ref, ids_ref, idr_ref, skip_ref, y_ref
):
    rows, width = x_ref.shape
    blocks = rows // STRETCH
    half = STRETCH // 2
    lane = lax.broadcasted_iota(jnp.int32, (STRETCH, 128), 1)
    first = lane < 64
    t_at = lax.broadcasted_iota(jnp.int32, (STRETCH, STRETCH), 0)
    s_at = lax.broadcasted_iota(jnp.int32, (STRETCH, STRETCH), 1)
    lower = s_at <= t_at
    for block in range(blocks):
        at = slice(block * STRETCH, (block + 1) * STRETCH)
        scores = lax.dot_general(
            c_ref[at], b_ref[at], (((1,), (1,)), ((), ())), preferred_element_type=F32
        )
        same = (ids_ref[at] == idr_ref[block : block + 1]) & lower
        scores = jnp.where(same, scores, 0.0)
        top, left, right = scores[:half, :half], scores[half:, :half], scores[half:, half:]
        for pair in range(width // 128):
            lanes = slice(pair * 128, (pair + 1) * 128)
            value = x_ref[at, lanes]
            upper_sum = lower_sum = None
            for which in range(2):
                head = 2 * pair + which
                keep = first if which == 0 else jnp.logical_not(first)
                mine = jnp.where(keep, value.astype(F32), 0.0).astype(BF16)
                col = col_ref[0, at, head : head + 1]
                row = row_ref[0, block, head : head + 1, :]
                m_top = top * jnp.exp2(jnp.minimum(col[:half] - row[:, :half], 80.0))
                m_left = left * jnp.exp2(col[half:] - row[:, :half])
                m_right = right * jnp.exp2(jnp.minimum(col[half:] - row[:, half:], 80.0))
                m_low = jnp.concatenate([m_left.astype(BF16), m_right.astype(BF16)], axis=1)
                up = jnp.dot(m_top.astype(BF16), mine[:half], preferred_element_type=F32)
                low = jnp.dot(m_low, mine, preferred_element_type=F32)
                upper_sum = up if which == 0 else upper_sum + up
                lower_sum = low if which == 0 else lower_sum + low
            skip = skip_ref[:, lanes]
            wide = value.astype(F32)
            y_ref[at.start : at.start + half, lanes] = upper_sum + skip * wide[:half]
            y_ref[at.start + half : at.stop, lanes] = lower_sum + skip * wide[half:]


def gate_kernel(
    y_ref, z_ref, c_ref, link_ref, expand_ref, enter_ref, inc_ref, row_gain_ref, out_ref, sq_ref
):
    rows, width = y_ref.shape
    blocks = rows // STRETCH

    @pl.when(pl.program_id(0) == 0)
    def _():
        sq_ref[...] = jnp.zeros_like(sq_ref)

    for tile in range(width // 256):
        lanes = slice(tile * 256, (tile + 1) * 256)
        state = enter_ref[0, :, lanes]
        for block in range(blocks):
            at = slice(block * STRETCH, (block + 1) * STRETCH)
            if block == 1:
                state = (
                    row_gain_ref[0:1, lanes] * state.astype(F32) + inc_ref[0, :, lanes]
                ).astype(BF16)
            inter = jnp.dot(c_ref[at], state, preferred_element_type=F32)
            link = jnp.dot(link_ref[0, at], expand_ref[:, lanes], preferred_element_type=F32)
            gate = silu(z_ref[at, lanes].astype(F32))
            gated = (y_ref[at, lanes] + inter * link) * gate
            out_ref[at, lanes] = gated
            square = gated * gated
            sq_ref[at] += square[:, :128] + square[:, 128:]


def norm_kernel(gated_ref, total_ref, gain_ref, out_ref, *, channels):
    scale = lax.rsqrt(total_ref[...] / channels + 1e-05)
    out_ref[...] = (gated_ref[...] * scale * gain_ref[...]).astype(BF16)


def split_two(value):
    high = value.astype(BF16)
    return jnp.concatenate([high, (value - high.astype(F32)).astype(BF16)], axis=-1)


def exchange(sums, groups):
    axis = "seq"
    count = lax.axis_size(axis)
    plane = count // 4
    mine = lax.axis_index(axis)
    place = mine % plane
    _, depth, width = sums.shape
    cut = groups * width // plane
    split = plane // groups
    chunks = sums.reshape(groups, depth, split, cut).transpose(0, 2, 1, 3)
    chunks = chunks.reshape(plane, depth, cut)

    def pick(array, index):
        return lax.dynamic_index_in_dim(array, index, 0, keepdims=False)

    def swap(array):
        got = [pick(array, place)]
        for k in range(1, plane):
            got.append(
                lax.ppermute(pick(array, place ^ k), axis, [(i, i ^ k) for i in range(count)])
            )
        return jnp.stack(got)

    came = swap(chunks)
    run = jnp.zeros((STATE, cut), F32)
    through = jnp.ones((1, cut), F32)
    entering, gains = [], []
    for source in range(plane):
        part = pick(came, place ^ source)
        gain = part[STATE : STATE + 1].astype(F32) + part[STATE + 1 : STATE + 2].astype(F32)
        entering.append(run)
        gains.append(through)
        run = gain * run + part[:STATE].astype(F32)
        through = through * gain
    before = lax.ppermute(
        run.astype(BF16), axis, [(i, i + plane) for i in range(count - plane)]
    ).astype(F32)
    ready = jnp.stack([(e + g * before).astype(BF16) for e, g in zip(entering, gains)])
    back = swap(ready)
    final = jnp.stack([pick(back, place ^ owner) for owner in range(plane)])
    final = final.reshape(groups, split, STATE, cut).transpose(0, 2, 1, 3)
    return final.reshape(groups, STATE, width)


def on_device(
    x_proj, bc_proj, z_proj, dt_raw, conv_x, conv_bc, bias_x, bias_bc, dt_bias, a_log,
    d_skip, norm_gain, seg_ids,
):
    rows, inner = x_proj.shape
    heads = dt_raw.shape[1]
    groups = bc_proj.shape[2] // STATE
    per = heads // groups
    size = inner // heads
    width = inner // groups
    blocks = rows // STRETCH
    seq = lax.axis_size("seq")
    bc_flat = bc_proj.reshape(rows, 2 * groups * STATE)
    wbc = conv_bc.reshape(4, 2 * groups * STATE)
    bbc = bias_bc.reshape(1, 2 * groups * STATE)
    route = [(i, i + 1) for i in range(seq - 1)]
    tail_ids = jnp.broadcast_to(seg_ids[rows - RIM :, None], (RIM, 128)).astype(BF16)
    ends = [
        x_proj[rows - RIM :],
        bc_proj[rows - RIM :].reshape(RIM, 2 * groups * STATE),
        tail_ids,
    ]
    rim = lax.ppermute(jnp.concatenate(ends, axis=1), "seq", route)
    rim_ids = rim[:, inner + 2 * groups * STATE].astype(jnp.int32)
    window_ids = jnp.concatenate([rim_ids, seg_ids])
    counted = jnp.stack(
        [(window_ids[RIM - 3 + k : RIM - 3 + k + rows] == seg_ids).astype(F32) for k in range(3)],
        axis=1,
    )

    step = jax.nn.softplus(dt_raw + dt_bias)
    rate = -jnp.exp(a_log) * LOG2E
    tri = jnp.tril(jnp.ones((STRETCH, STRETCH), F32))
    logs = (step * rate).reshape(blocks, STRETCH, heads)
    cum = jnp.einsum("ts,csh->cth", tri, logs, precision=lax.Precision.HIGHEST)
    last = cum[:, -1:]
    ids = seg_ids.reshape(blocks, STRETCH)
    before = window_ids[RIM - 1 : RIM - 1 + rows : STRETCH]
    steps = step.reshape(blocks, STRETCH, heads)
    tail = jnp.exp2(last - cum) * steps * (ids == ids[:, -1:]).astype(F32)[..., None]
    link = jnp.exp2(cum) * (ids == before[:, None]).astype(F32)[..., None]
    gain = jnp.exp2(last[:, 0]) * (ids[:, -1] == before).astype(F32)[:, None]

    def by_group(value):
        return value.reshape(rows, groups, per).transpose(1, 0, 2)

    tail_two = split_two(by_group(tail))
    link_two = split_two(by_group(link))
    col = by_group(cum)
    shifted = cum - jnp.log2(steps)
    row = shifted.reshape(blocks, STRETCH, groups, per).transpose(2, 0, 3, 1)
    row_gain = jnp.repeat(gain, size, axis=1)
    whole = row_gain[0] * row_gain[1]
    whole_high = whole.astype(BF16)
    whole_low = (whole - whole_high.astype(F32)).astype(BF16)
    gain_rows = jnp.stack([whole_high, whole_low]).reshape(2, groups, width).transpose(1, 0, 2)
    gain_rows = jnp.pad(gain_rows, ((0, 0), (0, 14), (0, 0)))
    expand = (
        lax.broadcasted_iota(jnp.int32, (2 * per, width), 0) % per
        == lax.broadcasted_iota(jnp.int32, (2 * per, width), 1) // size
    ).astype(BF16)

    params = pltpu.CompilerParams(vmem_limit_bytes=VMEM)
    wide = lambda n: pl.BlockSpec((n, width), lambda g: (0, g))
    state_b = lambda n: pl.BlockSpec((n, STATE), lambda g: (0, g))
    state_c = lambda n: pl.BlockSpec((n, STATE), lambda g: (0, g + groups))
    lead = lambda *shape: pl.BlockSpec((1,) + shape, lambda g: (g,) + (0,) * len(shape))
    tiles = inner // STATE
    rim_b = pl.BlockSpec((RIM, STATE), lambda g: (0, tiles + g))
    rim_c = pl.BlockSpec((RIM, STATE), lambda g: (0, tiles + groups + g))
    full = lambda *shape: pl.BlockSpec(shape, lambda g: (0,) * len(shape))
    bias_row = bias_x.reshape(1, inner)
    x_conv, b_conv, c_conv, inc, sums = pl.pallas_call(
        local_kernel,
        grid=(groups,),
        in_specs=[
            wide(rows), wide(RIM), state_b(rows), state_c(rows), rim_b, rim_c,
            wide(4), state_b(4), state_c(4), wide(1), state_b(1), state_c(1),
            full(rows, 3), lead(rows, 2 * per), lead(16, width), wide(blocks),
            full(2 * per, width),
        ],
        out_specs=[
            wide(rows), state_b(rows), state_b(rows), lead(STATE, width),
            lead(STATE + 16, width),
        ],
        out_shape=[
            jax.ShapeDtypeStruct((rows, inner), BF16),
            jax.ShapeDtypeStruct((rows, groups * STATE), BF16),
            jax.ShapeDtypeStruct((rows, groups * STATE), BF16),
            jax.ShapeDtypeStruct((groups, STATE, width), F32),
            jax.ShapeDtypeStruct((groups, STATE + 16, width), BF16),
        ],
        scratch_shapes=[
            pltpu.VMEM((width // 128, rows + RIM, 128), F32),
            pltpu.VMEM((rows + RIM, STATE), F32),
            pltpu.VMEM((rows + RIM, STATE), F32),
            pltpu.VMEM((rows, width), BF16),
            pltpu.VMEM((3, rows, 128), F32),
        ],
        compiler_params=params,
        cost_estimate=pl.CostEstimate(
            flops=4 * rows * inner * STATE, bytes_accessed=30 << 20, transcendentals=rows * inner
        ),
        name="local",
    )(
        x_proj, rim, bc_flat, bc_flat, rim, rim, conv_x, wbc, wbc, bias_row, bbc, bbc,
        counted, tail_two, gain_rows, row_gain, expand,
    )

    enter = exchange(sums, groups)

    y = pl.pallas_call(
        intra_kernel,
        grid=(groups,),
        in_specs=[
            wide(rows), state_b(rows), state_b(rows), lead(rows, per),
            lead(blocks, per, STRETCH), full(rows, 1), full(blocks, STRETCH), wide(1),
        ],
        out_specs=wide(rows),
        out_shape=jax.ShapeDtypeStruct((rows, inner), F32),
        compiler_params=params,
        cost_estimate=pl.CostEstimate(
            flops=40 * rows * inner * STRETCH, bytes_accessed=100 << 20,
            transcendentals=rows * heads * STRETCH,
        ),
        name="intra",
    )(
        x_conv, b_conv, c_conv, col, row, seg_ids.reshape(rows, 1), ids,
        jnp.repeat(d_skip, size).reshape(1, inner),
    )

    gated, squares = pl.pallas_call(
        gate_kernel,
        grid=(groups,),
        in_specs=[
            wide(rows), wide(rows), state_b(rows), lead(rows, 2 * per), full(2 * per, width),
            lead(STATE, width), lead(STATE, width), wide(blocks),
        ],
        out_specs=[wide(rows), full(rows, 128)],
        out_shape=[
            jax.ShapeDtypeStruct((rows, inner), F32),
            jax.ShapeDtypeStruct((rows, 128), F32),
        ],
        compiler_params=params,
        name="gate",
    )(y, z_proj, c_conv, link_two, expand, enter, inc, row_gain)

    total = jnp.sum(squares, axis=-1, keepdims=True)
    count = lax.axis_size("tp")
    own = total
    for k in range(1, count):
        total = total + lax.ppermute(own, "tp", [(i, (i + k) % count) for i in range(count)])
    part = rows // 4
    return pl.pallas_call(
        functools.partial(norm_kernel, channels=inner * count),
        grid=(4,),
        in_specs=[
            pl.BlockSpec((part, inner), lambda r: (r, 0)),
            pl.BlockSpec((part, 1), lambda r: (r, 0)),
            full(1, inner),
        ],
        out_specs=pl.BlockSpec((part, inner), lambda r: (r, 0)),
        out_shape=jax.ShapeDtypeStruct((rows, inner), BF16),
        compiler_params=params,
        name="norm",
    )(gated, total, norm_gain.reshape(1, inner))


def solution(mesh):
    in_specs = (
        P("seq", "tp"),
        P("seq", None, "tp"),
        P("seq", "tp"),
        P("seq", "tp"),
        P(None, "tp"),
        P(None, None, "tp"),
        P("tp"),
        P(None, "tp"),
        P("tp"),
        P("tp"),
        P("tp"),
        P("tp"),
        P("seq"),
    )
    return jax.shard_map(
        on_device, mesh=mesh, in_specs=in_specs, out_specs=P("seq", "tp"), check_vma=False
    )
```

```python
import functools

import jax
import jax.numpy as jnp
from jax import lax
from jax.experimental import pallas as pl
from jax.experimental.pallas import tpu as pltpu
from jax.sharding import PartitionSpec as P

STATE = 128
STRETCH = 256
RIM = 8
LOG2E = 1.4426950408889634
F32 = jnp.float32
BF16 = jnp.bfloat16
VMEM = 52 * 1024 * 1024


def silu(v):
    half = 0.5 * v
    return half * jnp.tanh(half) + half


def conv_tile(window, weight, bias, masks, start, rows):
    acc = jnp.broadcast_to(bias, (rows, 128))
    for tap in range(4):
        piece = window[pl.ds(RIM - 3 + tap + start, rows), :]
        term = piece * weight[tap : tap + 1]
        if tap < 3:
            term = term * masks[tap, pl.ds(start, rows), :]
        acc = acc + term
    return silu(acc).astype(BF16)


def selector(depth, width, start):
    row = lax.broadcasted_iota(jnp.int32, (depth, width), 0)
    lane = lax.broadcasted_iota(jnp.int32, (depth, width), 1) + start
    head = jnp.where(row >= depth // 2, row - depth // 2, row)
    low = head * 64
    return jnp.where((lane >= low) & (lane < low + 64), 1.0, 0.0).astype(BF16)


def local_kernel(
    x_ref, rim_ref, b_ref, c_ref, rimb_ref, rimc_ref, wx_ref, wb_ref, wc_ref,
    bx_ref, bb_ref, bc_ref, counted_ref, tail_ref, gain_ref, row_gain_ref,
    xo_ref, bo_ref, co_ref, inc_ref, sum_ref, window, window_b, window_c, weighted, masks, expand,
):
    rows, width = x_ref.shape
    blocks = rows // STRETCH

    @pl.when(pl.program_id(0) == 0)
    def _():
        for tap in range(3):
            masks[tap] = jnp.broadcast_to(counted_ref[:, tap : tap + 1], (rows, 128))

    expand[...] = selector(*expand.shape, pl.program_id(0) * width)
    window_b[0:RIM] = rimb_ref[...].astype(F32)
    window_c[0:RIM] = rimc_ref[...].astype(F32)
    window_b[RIM:] = b_ref[...].astype(F32)
    window_c[RIM:] = c_ref[...].astype(F32)
    for block in range(blocks):
        at = slice(block * STRETCH, (block + 1) * STRETCH)
        bo_ref[at] = conv_tile(
            window_b, wb_ref[...].astype(F32), bb_ref[...], masks, at.start, STRETCH
        )
        co_ref[at] = conv_tile(
            window_c, wc_ref[...].astype(F32), bc_ref[...], masks, at.start, STRETCH
        )
    for tile in range(width // 128):
        lanes = slice(tile * 128, (tile + 1) * 128)
        window[tile, 0:RIM] = rim_ref[:, lanes].astype(F32)
        window[tile, RIM:] = x_ref[:, lanes].astype(F32)
        weight = wx_ref[:, lanes].astype(F32)
        for block in range(blocks):
            at = slice(block * STRETCH, (block + 1) * STRETCH)
            value = conv_tile(
                window.at[tile], weight, bx_ref[:, lanes], masks, at.start, STRETCH
            )
            xo_ref[at, lanes] = value
            spread = jnp.dot(
                tail_ref[at, :], expand[:, lanes], preferred_element_type=F32
            )
            weighted[at, lanes] = (value.astype(F32) * spread).astype(BF16)
    parts = []
    for block in range(blocks):
        at = slice(block * STRETCH, (block + 1) * STRETCH)
        parts.append(
            lax.dot_general(
                bo_ref[at], weighted[at], (((0,), (0,)), ((), ())), preferred_element_type=F32
            )
        )
    inc_ref[0] = parts[0]
    sum_ref[0, 0:STATE] = (row_gain_ref[1:2] * parts[0] + parts[1]).astype(BF16)
    sum_ref[0, STATE:] = gain_ref[0]


def intra_kernel(
    x_ref, b_ref, c_ref, col_ref, row_ref, ids_ref, idr_ref, skip_ref,
    link_ref, inc_ref, y_ref, expand,
):
    rows, width = x_ref.shape
    blocks = rows // STRETCH
    half = STRETCH // 2
    lane = lax.broadcasted_iota(jnp.int32, (STRETCH, 128), 1)
    first = lane < 64
    t_at = lax.broadcasted_iota(jnp.int32, (STRETCH, STRETCH), 0)
    s_at = lax.broadcasted_iota(jnp.int32, (STRETCH, STRETCH), 1)
    lower = s_at <= t_at
    expand[...] = selector(*expand.shape, pl.program_id(0) * width)
    for block in range(blocks):
        at = slice(block * STRETCH, (block + 1) * STRETCH)
        scores = lax.dot_general(
            c_ref[at], b_ref[at], (((1,), (1,)), ((), ())), preferred_element_type=F32
        )
        same = (ids_ref[at] == idr_ref[block : block + 1]) & lower
        scores = jnp.where(same, scores, 0.0)
        top, left, right = scores[:half, :half], scores[half:, :half], scores[half:, half:]
        for pair in range(width // 128):
            lanes = slice(pair * 128, (pair + 1) * 128)
            value = x_ref[at, lanes]
            upper_sum = lower_sum = None
            for which in range(2):
                head = 2 * pair + which
                keep = first if which == 0 else jnp.logical_not(first)
                mine = jnp.where(keep, value.astype(F32), 0.0).astype(BF16)
                col = col_ref[0, at, head : head + 1]
                row = row_ref[0, block, head : head + 1, :]
                m_top = top * jnp.exp2(jnp.minimum(col[:half] - row[:, :half], 80.0))
                m_left = left * jnp.exp2(col[half:] - row[:, :half])
                m_right = right * jnp.exp2(jnp.minimum(col[half:] - row[:, half:], 80.0))
                m_low = jnp.concatenate([m_left.astype(BF16), m_right.astype(BF16)], axis=1)
                up = jnp.dot(m_top.astype(BF16), mine[:half], preferred_element_type=F32)
                low = jnp.dot(m_low, mine, preferred_element_type=F32)
                upper_sum = up if which == 0 else upper_sum + up
                lower_sum = low if which == 0 else lower_sum + low
            skip = skip_ref[:, lanes]
            wide = value.astype(F32)
            base = skip * wide
            if block == 1:
                carried = jnp.dot(
                    c_ref[at], inc_ref[0, :, lanes].astype(BF16), preferred_element_type=F32
                )
                link = jnp.dot(link_ref[at], expand[:, lanes], preferred_element_type=F32)
                base = base + carried * link
            y_ref[at.start : at.start + half, lanes] = upper_sum + base[:half]
            y_ref[at.start + half : at.stop, lanes] = lower_sum + base[half:]


def gate_kernel(y_ref, z_ref, c_ref, link_ref, enter_ref, out_ref, sq_ref, expand):
    rows, width = y_ref.shape
    expand[...] = selector(*expand.shape, pl.program_id(0) * width)

    @pl.when(pl.program_id(0) == 0)
    def _():
        sq_ref[...] = jnp.zeros_like(sq_ref)

    for tile in range(width // 256):
        lanes = slice(tile * 256, (tile + 1) * 256)
        for start in range(0, rows, STRETCH):
            at = slice(start, start + STRETCH)
            inter = jnp.dot(c_ref[at], enter_ref[0, :, lanes], preferred_element_type=F32)
            link = jnp.dot(link_ref[at], expand[:, lanes], preferred_element_type=F32)
            gate = silu(z_ref[at, lanes].astype(F32))
            gated = (y_ref[at, lanes] + inter * link) * gate
            out_ref[at, lanes] = gated
            square = gated * gated
            sq_ref[at] += square[:, :128] + square[:, 128:]


def norm_kernel(gated_ref, total_ref, gain_ref, out_ref, *, channels):
    scale = lax.rsqrt(total_ref[...] / channels + 1e-05)
    out_ref[...] = (gated_ref[...] * scale * gain_ref[...]).astype(BF16)


def split_two(value):
    high = value.astype(BF16)
    return jnp.concatenate([high, (value - high.astype(F32)).astype(BF16)], axis=-1)


def exchange(sums, groups, beside):
    axis = "seq"
    count = lax.axis_size(axis)
    plane = count // 4
    mine = lax.axis_index(axis)
    place = mine % plane
    _, depth, width = sums.shape
    cut = groups * width // plane
    split = plane // groups
    chunks = sums.reshape(groups, depth, split, cut).transpose(0, 2, 1, 3)
    chunks = chunks.reshape(plane, depth, cut)

    def pick(array, index):
        return lax.dynamic_index_in_dim(array, index, 0, keepdims=False)

    def swap(array):
        got = [pick(array, place)]
        for k in range(1, plane):
            got.append(
                lax.ppermute(pick(array, place ^ k), axis, [(i, i ^ k) for i in range(count)])
            )
        return jnp.stack(got)

    came, beside = lax.optimization_barrier((swap(chunks), beside))
    run = jnp.zeros((STATE, cut), F32)
    through = jnp.ones((1, cut), F32)
    entering, gains = [], []
    for source in range(plane):
        part = pick(came, place ^ source)
        gain = part[STATE : STATE + 1].astype(F32) + part[STATE + 1 : STATE + 2].astype(F32)
        entering.append(run)
        gains.append(through)
        run = gain * run + part[:STATE].astype(F32)
        through = through * gain
    before = lax.ppermute(
        run.astype(BF16), axis, [(i, i + plane) for i in range(count - plane)]
    ).astype(F32)
    ready = jnp.stack([(e + g * before).astype(BF16) for e, g in zip(entering, gains)])
    back = swap(ready)
    final = jnp.stack([pick(back, place ^ owner) for owner in range(plane)])
    final = final.reshape(groups, split, STATE, cut).transpose(0, 2, 1, 3)
    return final.reshape(groups, STATE, width), beside


def on_device(
    x_proj, bc_proj, z_proj, dt_raw, conv_x, conv_bc, bias_x, bias_bc, dt_bias, a_log,
    d_skip, norm_gain, seg_ids,
):
    rows, inner = x_proj.shape
    heads = dt_raw.shape[1]
    groups = bc_proj.shape[2] // STATE
    per = heads // groups
    size = inner // heads
    width = inner // groups
    blocks = rows // STRETCH
    seq = lax.axis_size("seq")
    bc_flat = bc_proj.reshape(rows, 2 * groups * STATE)
    wbc = conv_bc.reshape(4, 2 * groups * STATE)
    bbc = bias_bc.reshape(1, 2 * groups * STATE)
    route = [(i, i + 1) for i in range(seq - 1)]
    tail_ids = jnp.broadcast_to(seg_ids[rows - RIM :, None], (RIM, 128)).astype(BF16)
    ends = [
        x_proj[rows - RIM :],
        bc_proj[rows - RIM :].reshape(RIM, 2 * groups * STATE),
        tail_ids,
    ]
    rim = lax.ppermute(jnp.concatenate(ends, axis=1), "seq", route)
    rim_ids = rim[:, inner + 2 * groups * STATE].astype(jnp.int32)
    window_ids = jnp.concatenate([rim_ids, seg_ids])
    counted = jnp.stack(
        [(window_ids[RIM - 3 + k : RIM - 3 + k + rows] == seg_ids).astype(F32) for k in range(3)],
        axis=1,
    )

    step = jax.nn.softplus(dt_raw + dt_bias)
    rate = -jnp.exp(a_log) * LOG2E
    tri = jnp.tril(jnp.ones((STRETCH, STRETCH), F32))
    logs = (step * rate).reshape(blocks, STRETCH, heads)
    cum = jnp.einsum("ts,csh->cth", tri, logs, precision=lax.Precision.HIGHEST)
    last = cum[:, -1:]
    ids = seg_ids.reshape(blocks, STRETCH)
    before = window_ids[RIM - 1 : RIM - 1 + rows : STRETCH]
    steps = step.reshape(blocks, STRETCH, heads)
    tail = jnp.exp2(last - cum) * steps * (ids == ids[:, -1:]).astype(F32)[..., None]
    link = jnp.exp2(cum) * (ids == before[:, None]).astype(F32)[..., None]
    gain = jnp.exp2(last[:, 0]) * (ids[:, -1] == before).astype(F32)[:, None]

    def by_group(value):
        return value.reshape(rows, groups, per).transpose(1, 0, 2)

    flat = lambda value: split_two(value.reshape(rows, heads))
    tail_two, link_two = flat(tail), flat(link)
    reach = jnp.concatenate([jnp.ones_like(gain[:1]), gain[:1]])[:, None]
    reach_two = flat(link * reach)
    col = by_group(cum)
    shifted = cum - jnp.log2(steps)
    row = shifted.reshape(blocks, STRETCH, groups, per).transpose(2, 0, 3, 1)
    row_gain = jnp.repeat(gain, size, axis=1)
    whole = row_gain[0] * row_gain[1]
    whole_high = whole.astype(BF16)
    whole_low = (whole - whole_high.astype(F32)).astype(BF16)
    gain_rows = jnp.stack([whole_high, whole_low]).reshape(2, groups, width).transpose(1, 0, 2)
    gain_rows = jnp.pad(gain_rows, ((0, 0), (0, 14), (0, 0)))
    params = pltpu.CompilerParams(vmem_limit_bytes=VMEM)
    wide = lambda n: pl.BlockSpec((n, width), lambda g: (0, g))
    state_b = lambda n: pl.BlockSpec((n, STATE), lambda g: (0, g))
    state_c = lambda n: pl.BlockSpec((n, STATE), lambda g: (0, g + groups))
    lead = lambda *shape: pl.BlockSpec((1,) + shape, lambda g: (g,) + (0,) * len(shape))
    tiles = inner // STATE
    rim_b = pl.BlockSpec((RIM, STATE), lambda g: (0, tiles + g))
    rim_c = pl.BlockSpec((RIM, STATE), lambda g: (0, tiles + groups + g))
    full = lambda *shape: pl.BlockSpec(shape, lambda g: (0,) * len(shape))
    bias_row = bias_x.reshape(1, inner)
    x_conv, b_conv, c_conv, inc, sums = pl.pallas_call(
        local_kernel,
        grid=(groups,),
        in_specs=[
            wide(rows), wide(RIM), state_b(rows), state_c(rows), rim_b, rim_c,
            wide(4), state_b(4), state_c(4), wide(1), state_b(1), state_c(1),
            full(rows, 3), full(rows, 2 * heads), lead(16, width), wide(blocks),
        ],
        out_specs=[
            wide(rows), state_b(rows), state_b(rows), lead(STATE, width),
            lead(STATE + 16, width),
        ],
        out_shape=[
            jax.ShapeDtypeStruct((rows, inner), BF16),
            jax.ShapeDtypeStruct((rows, groups * STATE), BF16),
            jax.ShapeDtypeStruct((rows, groups * STATE), BF16),
            jax.ShapeDtypeStruct((groups, STATE, width), F32),
            jax.ShapeDtypeStruct((groups, STATE + 16, width), BF16),
        ],
        scratch_shapes=[
            pltpu.VMEM((width // 128, rows + RIM, 128), F32),
            pltpu.VMEM((rows + RIM, STATE), F32),
            pltpu.VMEM((rows + RIM, STATE), F32),
            pltpu.VMEM((rows, width), BF16),
            pltpu.VMEM((3, rows, 128), F32),
            pltpu.VMEM((2 * heads, width), BF16),
        ],
        compiler_params=params,
        cost_estimate=pl.CostEstimate(
            flops=4 * rows * inner * STATE, bytes_accessed=30 << 20, transcendentals=rows * inner
        ),
        name="local",
    )(
        x_proj, rim, bc_flat, bc_flat, rim, rim, conv_x, wbc, wbc, bias_row, bbc, bbc,
        counted, tail_two, gain_rows, row_gain,
    )

    y = pl.pallas_call(
        intra_kernel,
        grid=(groups,),
        in_specs=[
            wide(rows), state_b(rows), state_b(rows), lead(rows, per),
            lead(blocks, per, STRETCH), full(rows, 1), full(blocks, STRETCH), wide(1),
            full(rows, 2 * heads), lead(STATE, width),
        ],
        scratch_shapes=[pltpu.VMEM((2 * heads, width), BF16)],
        out_specs=wide(rows),
        out_shape=jax.ShapeDtypeStruct((rows, inner), F32),
        compiler_params=params,
        cost_estimate=pl.CostEstimate(
            flops=40 * rows * inner * STRETCH, bytes_accessed=100 << 20,
            transcendentals=rows * heads * STRETCH,
        ),
        name="intra",
    )(
        x_conv, b_conv, c_conv, col, row, seg_ids.reshape(rows, 1), ids,
        jnp.repeat(d_skip, size).reshape(1, inner), link_two, inc,
    )

    enter, y = exchange(sums, groups, y)

    narrow = width // 2
    slab = pl.BlockSpec((rows, narrow), lambda g: (0, g))
    gated, squares = pl.pallas_call(
        gate_kernel,
        grid=(2 * groups,),
        in_specs=[
            slab, slab, pl.BlockSpec((rows, STATE), lambda g: (0, g // 2)),
            full(rows, 2 * heads),
            pl.BlockSpec((1, STATE, narrow), lambda g: (g // 2, 0, g % 2)),
        ],
        out_specs=[slab, full(rows, 128)],
        out_shape=[
            jax.ShapeDtypeStruct((rows, inner), F32),
            jax.ShapeDtypeStruct((rows, 128), F32),
        ],
        scratch_shapes=[pltpu.VMEM((2 * heads, narrow), BF16)],
        compiler_params=params,
        name="gate",
    )(y, z_proj, c_conv, reach_two, enter)

    total = jnp.sum(squares, axis=-1, keepdims=True)
    count = lax.axis_size("tp")
    own = total
    for k in range(1, count):
        total = total + lax.ppermute(own, "tp", [(i, (i + k) % count) for i in range(count)])
    part = rows // 8
    return pl.pallas_call(
        functools.partial(norm_kernel, channels=inner * count),
        grid=(8,),
        in_specs=[
            pl.BlockSpec((part, inner), lambda r: (r, 0)),
            pl.BlockSpec((part, 1), lambda r: (r, 0)),
            full(1, inner),
        ],
        out_specs=pl.BlockSpec((part, inner), lambda r: (r, 0)),
        out_shape=jax.ShapeDtypeStruct((rows, inner), BF16),
        compiler_params=params,
        name="norm",
    )(gated, total, norm_gain.reshape(1, inner))


def solution(mesh):
    in_specs = (
        P("seq", "tp"),
        P("seq", None, "tp"),
        P("seq", "tp"),
        P("seq", "tp"),
        P(None, "tp"),
        P(None, None, "tp"),
        P("tp"),
        P(None, "tp"),
        P("tp"),
        P("tp"),
        P("tp"),
        P("tp"),
        P("seq"),
    )
    return jax.shard_map(
        on_device, mesh=mesh, in_specs=in_specs, out_specs=P("seq", "tp"), check_vma=False
    )
```

```python
import functools

import jax
import jax.numpy as jnp
from jax import lax
from jax.experimental import pallas as pl
from jax.experimental.pallas import tpu as pltpu
from jax.sharding import PartitionSpec as P

STATE = 128
STRETCH = 256
RIM = 8
LOG2E = 1.4426950408889634
F32 = jnp.float32
BF16 = jnp.bfloat16
VMEM = 52 * 1024 * 1024


def silu(v):
    half = 0.5 * v
    return half * jnp.tanh(half) + half


def conv_tile(window, weight, bias, masks, start, rows):
    acc = jnp.broadcast_to(bias, (rows, 128))
    for tap in range(4):
        piece = window[pl.ds(RIM - 3 + tap + start, rows), :]
        term = piece * weight[tap : tap + 1]
        if tap < 3:
            term = term * masks[tap, pl.ds(start, rows), :]
        acc = acc + term
    return silu(acc).astype(BF16)


def selector(depth, width, start):
    row = lax.broadcasted_iota(jnp.int32, (depth, width), 0)
    lane = lax.broadcasted_iota(jnp.int32, (depth, width), 1) + start
    head = jnp.where(row >= depth // 2, row - depth // 2, row)
    low = head * 64
    return jnp.where((lane >= low) & (lane < low + 64), 1.0, 0.0).astype(BF16)


def local_kernel(
    x_ref, rim_ref, b_ref, c_ref, rimb_ref, rimc_ref, wx_ref, wb_ref, wc_ref,
    bx_ref, bb_ref, bc_ref, counted_ref, tail_ref, gain_ref, row_gain_ref,
    xo_ref, bo_ref, co_ref, inc_ref, sum_ref, window, window_b, window_c, weighted, masks, expand,
):
    rows, width = x_ref.shape
    blocks = rows // STRETCH

    @pl.when(pl.program_id(0) == 0)
    def _():
        for tap in range(3):
            masks[tap] = jnp.broadcast_to(counted_ref[:, tap : tap + 1], (rows, 128))

    expand[...] = selector(*expand.shape, pl.program_id(0) * width)
    window_b[0:RIM] = rimb_ref[...].astype(F32)
    window_c[0:RIM] = rimc_ref[...].astype(F32)
    window_b[RIM:] = b_ref[...].astype(F32)
    window_c[RIM:] = c_ref[...].astype(F32)
    for block in range(blocks):
        at = slice(block * STRETCH, (block + 1) * STRETCH)
        bo_ref[at] = conv_tile(
            window_b, wb_ref[...].astype(F32), bb_ref[...], masks, at.start, STRETCH
        )
        co_ref[at] = conv_tile(
            window_c, wc_ref[...].astype(F32), bc_ref[...], masks, at.start, STRETCH
        )
    for tile in range(width // 128):
        lanes = slice(tile * 128, (tile + 1) * 128)
        window[tile, 0:RIM] = rim_ref[:, lanes].astype(F32)
        window[tile, RIM:] = x_ref[:, lanes].astype(F32)
        weight = wx_ref[:, lanes].astype(F32)
        for block in range(blocks):
            at = slice(block * STRETCH, (block + 1) * STRETCH)
            value = conv_tile(
                window.at[tile], weight, bx_ref[:, lanes], masks, at.start, STRETCH
            )
            xo_ref[at, lanes] = value
            spread = jnp.dot(
                tail_ref[at, :], expand[:, lanes], preferred_element_type=F32
            )
            weighted[at, lanes] = (value.astype(F32) * spread).astype(BF16)
    parts = []
    for block in range(blocks):
        at = slice(block * STRETCH, (block + 1) * STRETCH)
        parts.append(
            lax.dot_general(
                bo_ref[at], weighted[at], (((0,), (0,)), ((), ())), preferred_element_type=F32
            )
        )
    inc_ref[0] = parts[0]
    sum_ref[0, 0:STATE] = (row_gain_ref[1:2] * parts[0] + parts[1]).astype(BF16)
    sum_ref[0, STATE:] = gain_ref[0]


def intra_kernel(
    x_ref, b_ref, c_ref, col_ref, row_ref, ids_ref, idr_ref, skip_ref,
    link_ref, inc_ref, y_ref, expand,
):
    rows, width = x_ref.shape
    blocks = rows // STRETCH
    half = STRETCH // 2
    lane = lax.broadcasted_iota(jnp.int32, (STRETCH, 128), 1)
    first = lane < 64
    t_at = lax.broadcasted_iota(jnp.int32, (STRETCH, STRETCH), 0)
    s_at = lax.broadcasted_iota(jnp.int32, (STRETCH, STRETCH), 1)
    lower = s_at <= t_at
    expand[...] = selector(*expand.shape, pl.program_id(0) * width)
    for block in range(blocks):
        at = slice(block * STRETCH, (block + 1) * STRETCH)
        scores = lax.dot_general(
            c_ref[at], b_ref[at], (((1,), (1,)), ((), ())), preferred_element_type=F32
        )
        same = (ids_ref[at] == idr_ref[block : block + 1]) & lower
        scores = jnp.where(same, scores, 0.0)
        top, left, right = scores[:half, :half], scores[half:, :half], scores[half:, half:]
        for pair in range(width // 128):
            lanes = slice(pair * 128, (pair + 1) * 128)
            value = x_ref[at, lanes]
            upper_sum = lower_sum = None
            for which in range(2):
                head = 2 * pair + which
                keep = first if which == 0 else jnp.logical_not(first)
                mine = jnp.where(keep, value.astype(F32), 0.0).astype(BF16)
                col = col_ref[0, at, head : head + 1]
                row = row_ref[0, block, head : head + 1, :]
                m_top = top * jnp.exp2(jnp.minimum(col[:half] - row[:, :half], 80.0))
                m_left = left * jnp.exp2(col[half:] - row[:, :half])
                m_right = right * jnp.exp2(jnp.minimum(col[half:] - row[:, half:], 80.0))
                m_low = jnp.concatenate([m_left.astype(BF16), m_right.astype(BF16)], axis=1)
                up = jnp.dot(m_top.astype(BF16), mine[:half], preferred_element_type=F32)
                low = jnp.dot(m_low, mine, preferred_element_type=F32)
                upper_sum = up if which == 0 else upper_sum + up
                lower_sum = low if which == 0 else lower_sum + low
            skip = skip_ref[:, lanes]
            wide = value.astype(F32)
            base = skip * wide
            if block == 1:
                carried = jnp.dot(
                    c_ref[at], inc_ref[0, :, lanes].astype(BF16), preferred_element_type=F32
                )
                link = jnp.dot(link_ref[at], expand[:, lanes], preferred_element_type=F32)
                base = base + carried * link
            y_ref[at.start : at.start + half, lanes] = upper_sum + base[:half]
            y_ref[at.start + half : at.stop, lanes] = lower_sum + base[half:]


def gate_kernel(y_ref, z_ref, c_ref, link_ref, enter_ref, out_ref, sq_ref, expand):
    rows, width = y_ref.shape
    expand[...] = selector(*expand.shape, pl.program_id(0) * width)

    @pl.when(pl.program_id(0) == 0)
    def _():
        sq_ref[...] = jnp.zeros_like(sq_ref)

    for tile in range(width // 256):
        lanes = slice(tile * 256, (tile + 1) * 256)
        for start in range(0, rows, STRETCH):
            at = slice(start, start + STRETCH)
            inter = jnp.dot(c_ref[at], enter_ref[0, :, lanes], preferred_element_type=F32)
            link = jnp.dot(link_ref[at], expand[:, lanes], preferred_element_type=F32)
            gate = silu(z_ref[at, lanes].astype(F32))
            gated = (y_ref[at, lanes] + inter * link) * gate
            out_ref[at, lanes] = gated
            square = gated * gated
            sq_ref[at] += square[:, :128] + square[:, 128:]


def norm_kernel(gated_ref, total_ref, gain_ref, out_ref, *, channels):
    part = out_ref.shape[0]
    total = total_ref[pl.ds(pl.multiple_of(pl.program_id(0) * part, part), part), :]
    scale = lax.rsqrt(total / channels + 1e-05)
    out_ref[...] = (gated_ref[...] * scale * gain_ref[...]).astype(BF16)


def split_two(value):
    high = value.astype(BF16)
    return jnp.concatenate([high, (value - high.astype(F32)).astype(BF16)], axis=-1)


def exchange(sums, groups, beside):
    axis = "seq"
    count = lax.axis_size(axis)
    plane = count // 4
    mine = lax.axis_index(axis)
    place = mine % plane
    _, depth, width = sums.shape
    cut = groups * width // plane
    split = plane // groups
    chunks = sums.reshape(groups, depth, split, cut).transpose(0, 2, 1, 3)
    chunks = chunks.reshape(plane, depth, cut)

    def pick(array, index):
        return lax.dynamic_index_in_dim(array, index, 0, keepdims=False)

    def swap(array):
        got = [pick(array, place)]
        for k in range(1, plane):
            got.append(
                lax.ppermute(pick(array, place ^ k), axis, [(i, i ^ k) for i in range(count)])
            )
        return jnp.stack(got)

    came, beside = lax.optimization_barrier((swap(chunks), beside))
    run = jnp.zeros((STATE, cut), F32)
    through = jnp.ones((1, cut), F32)
    entering, gains = [], []
    for source in range(plane):
        part = pick(came, place ^ source)
        gain = part[STATE : STATE + 1].astype(F32) + part[STATE + 1 : STATE + 2].astype(F32)
        entering.append(run)
        gains.append(through)
        run = gain * run + part[:STATE].astype(F32)
        through = through * gain
    before = lax.ppermute(
        run.astype(BF16), axis, [(i, i + plane) for i in range(count - plane)]
    ).astype(F32)
    ready = jnp.stack([(e + g * before).astype(BF16) for e, g in zip(entering, gains)])
    back = swap(ready)
    final = jnp.stack([pick(back, place ^ owner) for owner in range(plane)])
    final = final.reshape(groups, split, STATE, cut).transpose(0, 2, 1, 3)
    return final.reshape(groups, STATE, width), beside


def on_device(
    x_proj, bc_proj, z_proj, dt_raw, conv_x, conv_bc, bias_x, bias_bc, dt_bias, a_log,
    d_skip, norm_gain, seg_ids,
):
    rows, inner = x_proj.shape
    heads = dt_raw.shape[1]
    groups = bc_proj.shape[2] // STATE
    per = heads // groups
    size = inner // heads
    width = inner // groups
    blocks = rows // STRETCH
    seq = lax.axis_size("seq")
    bc_flat = bc_proj.reshape(rows, 2 * groups * STATE)
    wbc = conv_bc.reshape(4, 2 * groups * STATE)
    bbc = bias_bc.reshape(1, 2 * groups * STATE)
    route = [(i, i + 1) for i in range(seq - 1)]
    tail_ids = jnp.broadcast_to(seg_ids[rows - RIM :, None], (RIM, 128)).astype(BF16)
    ends = [
        x_proj[rows - RIM :],
        bc_proj[rows - RIM :].reshape(RIM, 2 * groups * STATE),
        tail_ids,
    ]
    rim = lax.ppermute(jnp.concatenate(ends, axis=1), "seq", route)
    rim_ids = rim[:, inner + 2 * groups * STATE].astype(jnp.int32)
    window_ids = jnp.concatenate([rim_ids, seg_ids])
    counted = jnp.stack(
        [(window_ids[RIM - 3 + k : RIM - 3 + k + rows] == seg_ids).astype(F32) for k in range(3)],
        axis=1,
    )

    step = jax.nn.softplus(dt_raw + dt_bias)
    rate = -jnp.exp(a_log) * LOG2E
    tri = jnp.tril(jnp.ones((STRETCH, STRETCH), F32))
    logs = (step * rate).reshape(blocks, STRETCH, heads)
    cum = jnp.einsum("ts,csh->cth", tri, logs, precision=lax.Precision.HIGHEST)
    last = cum[:, -1:]
    ids = seg_ids.reshape(blocks, STRETCH)
    before = window_ids[RIM - 1 : RIM - 1 + rows : STRETCH]
    steps = step.reshape(blocks, STRETCH, heads)
    tail = jnp.exp2(last - cum) * steps * (ids == ids[:, -1:]).astype(F32)[..., None]
    link = jnp.exp2(cum) * (ids == before[:, None]).astype(F32)[..., None]
    gain = jnp.exp2(last[:, 0]) * (ids[:, -1] == before).astype(F32)[:, None]

    def by_group(value):
        return value.reshape(rows, groups, per).transpose(1, 0, 2)

    flat = lambda value: split_two(value.reshape(rows, heads))
    tail_two, link_two = flat(tail), flat(link)
    reach = jnp.concatenate([jnp.ones_like(gain[:1]), gain[:1]])[:, None]
    reach_two = flat(link * reach)
    col = by_group(cum)
    shifted = cum - jnp.log2(steps)
    row = shifted.reshape(blocks, STRETCH, groups, per).transpose(2, 0, 3, 1)
    row_gain = jnp.repeat(gain, size, axis=1)
    whole = row_gain[0] * row_gain[1]
    whole_high = whole.astype(BF16)
    whole_low = (whole - whole_high.astype(F32)).astype(BF16)
    gain_rows = jnp.stack([whole_high, whole_low]).reshape(2, groups, width).transpose(1, 0, 2)
    gain_rows = jnp.pad(gain_rows, ((0, 0), (0, 14), (0, 0)))
    params = pltpu.CompilerParams(vmem_limit_bytes=VMEM)
    wide = lambda n: pl.BlockSpec((n, width), lambda g: (0, g))
    state_b = lambda n: pl.BlockSpec((n, STATE), lambda g: (0, g))
    state_c = lambda n: pl.BlockSpec((n, STATE), lambda g: (0, g + groups))
    lead = lambda *shape: pl.BlockSpec((1,) + shape, lambda g: (g,) + (0,) * len(shape))
    tiles = inner // STATE
    rim_b = pl.BlockSpec((RIM, STATE), lambda g: (0, tiles + g))
    rim_c = pl.BlockSpec((RIM, STATE), lambda g: (0, tiles + groups + g))
    full = lambda *shape: pl.BlockSpec(shape, lambda g: (0,) * len(shape))
    bias_row = bias_x.reshape(1, inner)
    x_conv, b_conv, c_conv, inc, sums = pl.pallas_call(
        local_kernel,
        grid=(groups,),
        in_specs=[
            wide(rows), wide(RIM), state_b(rows), state_c(rows), rim_b, rim_c,
            wide(4), state_b(4), state_c(4), wide(1), state_b(1), state_c(1),
            full(rows, 3), full(rows, 2 * heads), lead(16, width), wide(blocks),
        ],
        out_specs=[
            wide(rows), state_b(rows), state_b(rows), lead(STATE, width),
            lead(STATE + 16, width),
        ],
        out_shape=[
            jax.ShapeDtypeStruct((rows, inner), BF16),
            jax.ShapeDtypeStruct((rows, groups * STATE), BF16),
            jax.ShapeDtypeStruct((rows, groups * STATE), BF16),
            jax.ShapeDtypeStruct((groups, STATE, width), F32),
            jax.ShapeDtypeStruct((groups, STATE + 16, width), BF16),
        ],
        scratch_shapes=[
            pltpu.VMEM((width // 128, rows + RIM, 128), F32),
            pltpu.VMEM((rows + RIM, STATE), F32),
            pltpu.VMEM((rows + RIM, STATE), F32),
            pltpu.VMEM((rows, width), BF16),
            pltpu.VMEM((3, rows, 128), F32),
            pltpu.VMEM((2 * heads, width), BF16),
        ],
        compiler_params=params,
        cost_estimate=pl.CostEstimate(
            flops=4 * rows * inner * STATE, bytes_accessed=30 << 20, transcendentals=rows * inner
        ),
        name="local",
    )(
        x_proj, rim, bc_flat, bc_flat, rim, rim, conv_x, wbc, wbc, bias_row, bbc, bbc,
        counted, tail_two, gain_rows, row_gain,
    )

    y = pl.pallas_call(
        intra_kernel,
        grid=(groups,),
        in_specs=[
            wide(rows), state_b(rows), state_b(rows), lead(rows, per),
            lead(blocks, per, STRETCH), full(rows, 1), full(blocks, STRETCH), wide(1),
            full(rows, 2 * heads), lead(STATE, width),
        ],
        scratch_shapes=[pltpu.VMEM((2 * heads, width), BF16)],
        out_specs=wide(rows),
        out_shape=jax.ShapeDtypeStruct((rows, inner), F32),
        compiler_params=params,
        cost_estimate=pl.CostEstimate(
            flops=40 * rows * inner * STRETCH, bytes_accessed=100 << 20,
            transcendentals=rows * heads * STRETCH,
        ),
        name="intra",
    )(
        x_conv, b_conv, c_conv, col, row, seg_ids.reshape(rows, 1), ids,
        jnp.repeat(d_skip, size).reshape(1, inner), link_two, inc,
    )

    enter, y = exchange(sums, groups, y)

    gated, squares = pl.pallas_call(
        gate_kernel,
        grid=(groups,),
        in_specs=[
            wide(rows), wide(rows), state_b(rows), full(rows, 2 * heads), lead(STATE, width),
        ],
        out_specs=[wide(rows), full(rows, 128)],
        out_shape=[
            jax.ShapeDtypeStruct((rows, inner), F32),
            jax.ShapeDtypeStruct((rows, 128), F32),
        ],
        scratch_shapes=[pltpu.VMEM((2 * heads, width), BF16)],
        compiler_params=params,
        name="gate",
    )(y, z_proj, c_conv, reach_two, enter)

    total = jnp.sum(squares, axis=-1, keepdims=True)
    count = lax.axis_size("tp")
    own = total
    for k in range(1, count):
        total = total + lax.ppermute(own, "tp", [(i, (i + k) % count) for i in range(count)])
    part = rows // 4
    return pl.pallas_call(
        functools.partial(norm_kernel, channels=inner * count),
        grid=(4,),
        in_specs=[
            pl.BlockSpec((part, inner), lambda r: (r, 0)),
            full(rows, 1),
            full(1, inner),
        ],
        out_specs=pl.BlockSpec((part, inner), lambda r: (r, 0)),
        out_shape=jax.ShapeDtypeStruct((rows, inner), BF16),
        compiler_params=params,
        name="norm",
    )(gated, total, norm_gain.reshape(1, inner))


def solution(mesh):
    in_specs = (
        P("seq", "tp"),
        P("seq", None, "tp"),
        P("seq", "tp"),
        P("seq", "tp"),
        P(None, "tp"),
        P(None, None, "tp"),
        P("tp"),
        P(None, "tp"),
        P("tp"),
        P("tp"),
        P("tp"),
        P("tp"),
        P("seq"),
    )
    return jax.shard_map(
        on_device, mesh=mesh, in_specs=in_specs, out_specs=P("seq", "tp"), check_vma=False
    )
```

```python
import functools

import jax
import jax.numpy as jnp
from jax import lax
from jax.experimental import pallas as pl
from jax.experimental.pallas import tpu as pltpu
from jax.sharding import PartitionSpec as P

STATE = 128
STRETCH = 256
RIM = 8
LOG2E = 1.4426950408889634
F32 = jnp.float32
BF16 = jnp.bfloat16
VMEM = 52 * 1024 * 1024


def silu(v):
    half = 0.5 * v
    return half * jnp.tanh(half) + half


def conv_tile(window, weight, bias, masks, start, rows):
    acc = jnp.broadcast_to(bias, (rows, 128))
    for tap in range(4):
        piece = window[pl.ds(RIM - 3 + tap + start, rows), :]
        term = piece * weight[tap : tap + 1]
        if tap < 3:
            term = term * masks[tap, pl.ds(start, rows), :]
        acc = acc + term
    return silu(acc).astype(BF16)


def selector(depth, width, start):
    row = lax.broadcasted_iota(jnp.int32, (depth, width), 0)
    lane = lax.broadcasted_iota(jnp.int32, (depth, width), 1) + start
    head = jnp.where(row >= depth // 2, row - depth // 2, row)
    low = head * 64
    return jnp.where((lane >= low) & (lane < low + 64), 1.0, 0.0).astype(BF16)


def local_kernel(
    x_ref, rim_ref, b_ref, c_ref, rimb_ref, rimc_ref, wx_ref, wb_ref, wc_ref,
    bx_ref, bb_ref, bc_ref, counted_ref, tail_ref, gain_ref, row_gain_ref,
    xo_ref, bo_ref, co_ref, inc_ref, sum_ref, window, window_b, window_c, weighted, masks, expand,
):
    rows, width = x_ref.shape
    blocks = rows // STRETCH

    @pl.when(pl.program_id(0) == 0)
    def _():
        for tap in range(3):
            masks[tap] = jnp.broadcast_to(counted_ref[:, tap : tap + 1], (rows, 128))

    expand[...] = selector(*expand.shape, pl.program_id(0) * width)
    window_b[0:RIM] = rimb_ref[...].astype(F32)
    window_c[0:RIM] = rimc_ref[...].astype(F32)
    window_b[RIM:] = b_ref[...].astype(F32)
    window_c[RIM:] = c_ref[...].astype(F32)
    for block in range(blocks):
        at = slice(block * STRETCH, (block + 1) * STRETCH)
        bo_ref[at] = conv_tile(
            window_b, wb_ref[...].astype(F32), bb_ref[...], masks, at.start, STRETCH
        )
        co_ref[at] = conv_tile(
            window_c, wc_ref[...].astype(F32), bc_ref[...], masks, at.start, STRETCH
        )
    for tile in range(width // 128):
        lanes = slice(tile * 128, (tile + 1) * 128)
        window[tile, 0:RIM] = rim_ref[:, lanes].astype(F32)
        window[tile, RIM:] = x_ref[:, lanes].astype(F32)
        weight = wx_ref[:, lanes].astype(F32)
        for block in range(blocks):
            at = slice(block * STRETCH, (block + 1) * STRETCH)
            value = conv_tile(
                window.at[tile], weight, bx_ref[:, lanes], masks, at.start, STRETCH
            )
            xo_ref[at, lanes] = value
            spread = jnp.dot(
                tail_ref[at, :], expand[:, lanes], preferred_element_type=F32
            )
            weighted[at, lanes] = (value.astype(F32) * spread).astype(BF16)
    parts = []
    for block in range(blocks):
        at = slice(block * STRETCH, (block + 1) * STRETCH)
        parts.append(
            lax.dot_general(
                bo_ref[at], weighted[at], (((0,), (0,)), ((), ())), preferred_element_type=F32
            )
        )
    inc_ref[0] = parts[0]
    sum_ref[0, 0:STATE] = (row_gain_ref[1:2] * parts[0] + parts[1]).astype(BF16)
    sum_ref[0, STATE:] = gain_ref[0]


def intra_kernel(
    x_ref, b_ref, c_ref, col_ref, row_ref, ids_ref, idr_ref, skip_ref,
    link_ref, inc_ref, y_ref, expand,
):
    rows, width = x_ref.shape
    blocks = rows // STRETCH
    half = STRETCH // 2
    lane = lax.broadcasted_iota(jnp.int32, (STRETCH, 128), 1)
    first = lane < 64
    t_at = lax.broadcasted_iota(jnp.int32, (STRETCH, STRETCH), 0)
    s_at = lax.broadcasted_iota(jnp.int32, (STRETCH, STRETCH), 1)
    lower = s_at <= t_at
    expand[...] = selector(*expand.shape, pl.program_id(0) * width)
    for block in range(blocks):
        at = slice(block * STRETCH, (block + 1) * STRETCH)
        scores = lax.dot_general(
            c_ref[at], b_ref[at], (((1,), (1,)), ((), ())), preferred_element_type=F32
        )
        same = (ids_ref[at] == idr_ref[block : block + 1]) & lower
        scores = jnp.where(same, scores, 0.0)
        top, left, right = scores[:half, :half], scores[half:, :half], scores[half:, half:]
        for pair in range(width // 128):
            lanes = slice(pair * 128, (pair + 1) * 128)
            value = x_ref[at, lanes]
            upper_sum = lower_sum = None
            for which in range(2):
                head = 2 * pair + which
                keep = first if which == 0 else jnp.logical_not(first)
                mine = jnp.where(keep, value.astype(F32), 0.0).astype(BF16)
                col = col_ref[0, at, head : head + 1]
                row = row_ref[0, block, head : head + 1, :]
                m_top = top * jnp.exp2(jnp.minimum(col[:half] - row[:, :half], 80.0))
                m_left = left * jnp.exp2(col[half:] - row[:, :half])
                m_right = right * jnp.exp2(jnp.minimum(col[half:] - row[:, half:], 80.0))
                m_low = jnp.concatenate([m_left.astype(BF16), m_right.astype(BF16)], axis=1)
                up = jnp.dot(m_top.astype(BF16), mine[:half], preferred_element_type=F32)
                low = jnp.dot(m_low, mine, preferred_element_type=F32)
                upper_sum = up if which == 0 else upper_sum + up
                lower_sum = low if which == 0 else lower_sum + low
            skip = skip_ref[:, lanes]
            wide = value.astype(F32)
            base = skip * wide
            if block == 1:
                carried = jnp.dot(
                    c_ref[at], inc_ref[0, :, lanes].astype(BF16), preferred_element_type=F32
                )
                link = jnp.dot(link_ref[at], expand[:, lanes], preferred_element_type=F32)
                base = base + carried * link
            y_ref[at.start : at.start + half, lanes] = upper_sum + base[:half]
            y_ref[at.start + half : at.stop, lanes] = lower_sum + base[half:]


def gate_kernel(y_ref, z_ref, c_ref, link_ref, enter_ref, out_ref, sq_ref, expand):
    rows, width = y_ref.shape
    expand[...] = selector(*expand.shape, pl.program_id(0) * width)

    @pl.when(pl.program_id(0) == 0)
    def _():
        sq_ref[...] = jnp.zeros_like(sq_ref)

    for tile in range(width // 256):
        lanes = slice(tile * 256, (tile + 1) * 256)
        for start in range(0, rows, STRETCH):
            at = slice(start, start + STRETCH)
            inter = jnp.dot(c_ref[at], enter_ref[0, :, lanes], preferred_element_type=F32)
            link = jnp.dot(link_ref[at], expand[:, lanes], preferred_element_type=F32)
            gate = silu(z_ref[at, lanes].astype(F32))
            gated = (y_ref[at, lanes] + inter * link) * gate
            out_ref[at, lanes] = gated
            square = gated * gated
            sq_ref[at] += square[:, :128] + square[:, 128:]


def norm_kernel(gated_ref, total_ref, gain_ref, out_ref, *, channels):
    part = out_ref.shape[0]
    total = total_ref[pl.ds(pl.multiple_of(pl.program_id(0) * part, part), part), :]
    scale = lax.rsqrt(total / channels + 1e-05)
    out_ref[...] = (gated_ref[...] * scale * gain_ref[...]).astype(BF16)


def split_two(value):
    high = value.astype(BF16)
    return jnp.concatenate([high, (value - high.astype(F32)).astype(BF16)], axis=-1)


def exchange(sums, groups, beside):
    axis = "seq"
    count = lax.axis_size(axis)
    plane = count // 4
    mine = lax.axis_index(axis)
    place = mine % plane
    _, depth, width = sums.shape
    cut = groups * width // plane
    split = plane // groups
    chunks = sums.reshape(groups, depth, split, cut).transpose(0, 2, 1, 3)
    chunks = chunks.reshape(plane, depth, cut)

    def pick(array, index):
        return lax.dynamic_index_in_dim(array, index, 0, keepdims=False)

    def swap(array):
        got = [pick(array, place)]
        for k in range(1, plane):
            got.append(
                lax.ppermute(pick(array, place ^ k), axis, [(i, i ^ k) for i in range(count)])
            )
        return jnp.stack(got)

    came, beside = lax.optimization_barrier((swap(chunks), beside))
    run = jnp.zeros((STATE, cut), F32)
    through = jnp.ones((1, cut), F32)
    entering, gains = [], []
    for source in range(plane):
        part = pick(came, place ^ source)
        gain = part[STATE : STATE + 1].astype(F32) + part[STATE + 1 : STATE + 2].astype(F32)
        entering.append(run)
        gains.append(through)
        run = gain * run + part[:STATE].astype(F32)
        through = through * gain
    before = lax.ppermute(
        run.astype(BF16), axis, [(i, i + plane) for i in range(count - plane)]
    ).astype(F32)
    ready = jnp.stack([(e + g * before).astype(BF16) for e, g in zip(entering, gains)])
    back = swap(ready)
    final = jnp.stack([pick(back, place ^ owner) for owner in range(plane)])
    final = final.reshape(groups, split, STATE, cut).transpose(0, 2, 1, 3)
    return final.reshape(groups, STATE, width), beside


def on_device(
    x_proj, bc_proj, z_proj, dt_raw, conv_x, conv_bc, bias_x, bias_bc, dt_bias, a_log,
    d_skip, norm_gain, seg_ids,
):
    rows, inner = x_proj.shape
    heads = dt_raw.shape[1]
    groups = bc_proj.shape[2] // STATE
    per = heads // groups
    size = inner // heads
    width = inner // groups
    blocks = rows // STRETCH
    seq = lax.axis_size("seq")
    bc_flat = bc_proj.reshape(rows, 2 * groups * STATE)
    wbc = conv_bc.reshape(4, 2 * groups * STATE)
    bbc = bias_bc.reshape(1, 2 * groups * STATE)
    route = [(i, i + 1) for i in range(seq - 1)]
    tail_ids = jnp.broadcast_to(seg_ids[rows - RIM :, None], (RIM, 128)).astype(BF16)
    ends = [
        x_proj[rows - RIM :],
        bc_proj[rows - RIM :].reshape(RIM, 2 * groups * STATE),
        tail_ids,
    ]
    rim = lax.ppermute(jnp.concatenate(ends, axis=1), "seq", route)
    rim_ids = rim[:, inner + 2 * groups * STATE].astype(jnp.int32)
    window_ids = jnp.concatenate([rim_ids, seg_ids])
    counted = jnp.stack(
        [(window_ids[RIM - 3 + k : RIM - 3 + k + rows] == seg_ids).astype(F32) for k in range(3)],
        axis=1,
    )

    step = jax.nn.softplus(dt_raw + dt_bias)
    rate = -jnp.exp(a_log) * LOG2E
    tri = jnp.tril(jnp.ones((STRETCH, STRETCH), F32))
    logs = (step * rate).reshape(blocks, STRETCH, heads)
    cum = jnp.einsum("ts,csh->cth", tri, logs, precision=lax.Precision.HIGHEST)
    last = cum[:, -1:]
    ids = seg_ids.reshape(blocks, STRETCH)
    before = window_ids[RIM - 1 : RIM - 1 + rows : STRETCH]
    steps = step.reshape(blocks, STRETCH, heads)
    tail = jnp.exp2(last - cum) * steps * (ids == ids[:, -1:]).astype(F32)[..., None]
    link = jnp.exp2(cum) * (ids == before[:, None]).astype(F32)[..., None]
    gain = jnp.exp2(last[:, 0]) * (ids[:, -1] == before).astype(F32)[:, None]

    def by_group(value):
        return value.reshape(rows, groups, per).transpose(1, 0, 2)

    flat = lambda value: split_two(value.reshape(rows, heads))
    tail_two, link_two = flat(tail), flat(link)
    reach = jnp.concatenate([jnp.ones_like(gain[:1]), gain[:1]])[:, None]
    reach_two = flat(link * reach)
    col = by_group(cum)
    shifted = cum - jnp.log2(steps)
    row = shifted.reshape(blocks, STRETCH, groups, per).transpose(2, 0, 3, 1)
    row_gain = jnp.repeat(gain, size, axis=1)
    whole = row_gain[0] * row_gain[1]
    whole_high = whole.astype(BF16)
    whole_low = (whole - whole_high.astype(F32)).astype(BF16)
    gain_rows = jnp.stack([whole_high, whole_low]).reshape(2, groups, width).transpose(1, 0, 2)
    gain_rows = jnp.pad(gain_rows, ((0, 0), (0, 14), (0, 0)))
    params = pltpu.CompilerParams(vmem_limit_bytes=VMEM)
    wide = lambda n: pl.BlockSpec((n, width), lambda g: (0, g))
    state_b = lambda n: pl.BlockSpec((n, STATE), lambda g: (0, g))
    state_c = lambda n: pl.BlockSpec((n, STATE), lambda g: (0, g + groups))
    lead = lambda *shape: pl.BlockSpec((1,) + shape, lambda g: (g,) + (0,) * len(shape))
    tiles = inner // STATE
    rim_b = pl.BlockSpec((RIM, STATE), lambda g: (0, tiles + g))
    rim_c = pl.BlockSpec((RIM, STATE), lambda g: (0, tiles + groups + g))
    full = lambda *shape: pl.BlockSpec(shape, lambda g: (0,) * len(shape))
    bias_row = bias_x.reshape(1, inner)
    x_conv, b_conv, c_conv, inc, sums = pl.pallas_call(
        local_kernel,
        grid=(groups,),
        in_specs=[
            wide(rows), wide(RIM), state_b(rows), state_c(rows), rim_b, rim_c,
            wide(4), state_b(4), state_c(4), wide(1), state_b(1), state_c(1),
            full(rows, 3), full(rows, 2 * heads), lead(16, width), wide(blocks),
        ],
        out_specs=[
            wide(rows), state_b(rows), state_b(rows), lead(STATE, width),
            lead(STATE + 16, width),
        ],
        out_shape=[
            jax.ShapeDtypeStruct((rows, inner), BF16),
            jax.ShapeDtypeStruct((rows, groups * STATE), BF16),
            jax.ShapeDtypeStruct((rows, groups * STATE), BF16),
            jax.ShapeDtypeStruct((groups, STATE, width), F32),
            jax.ShapeDtypeStruct((groups, STATE + 16, width), BF16),
        ],
        scratch_shapes=[
            pltpu.VMEM((width // 128, rows + RIM, 128), F32),
            pltpu.VMEM((rows + RIM, STATE), F32),
            pltpu.VMEM((rows + RIM, STATE), F32),
            pltpu.VMEM((rows, width), BF16),
            pltpu.VMEM((3, rows, 128), F32),
            pltpu.VMEM((2 * heads, width), BF16),
        ],
        compiler_params=params,
        cost_estimate=pl.CostEstimate(
            flops=4 * rows * inner * STATE, bytes_accessed=30 << 20, transcendentals=rows * inner
        ),
        name="local",
    )(
        x_proj, rim, bc_flat, bc_flat, rim, rim, conv_x, wbc, wbc, bias_row, bbc, bbc,
        counted, tail_two, gain_rows, row_gain,
    )

    y = pl.pallas_call(
        intra_kernel,
        grid=(groups,),
        in_specs=[
            wide(rows), state_b(rows), state_b(rows), lead(rows, per),
            lead(blocks, per, STRETCH), full(rows, 1), full(blocks, STRETCH), wide(1),
            full(rows, 2 * heads), lead(STATE, width),
        ],
        scratch_shapes=[pltpu.VMEM((2 * heads, width), BF16)],
        out_specs=wide(rows),
        out_shape=jax.ShapeDtypeStruct((rows, inner), F32),
        compiler_params=params,
        cost_estimate=pl.CostEstimate(
            flops=40 * rows * inner * STRETCH, bytes_accessed=100 << 20,
            transcendentals=rows * heads * STRETCH,
        ),
        name="intra",
    )(
        x_conv, b_conv, c_conv, col, row, seg_ids.reshape(rows, 1), ids,
        jnp.repeat(d_skip, size).reshape(1, inner), link_two, inc,
    )

    enter, y = exchange(sums, groups, y)

    gated, squares = pl.pallas_call(
        gate_kernel,
        grid=(groups,),
        in_specs=[
            wide(rows), wide(rows), state_b(rows), full(rows, 2 * heads), lead(STATE, width),
        ],
        out_specs=[wide(rows), full(rows, 128)],
        out_shape=[
            jax.ShapeDtypeStruct((rows, inner), F32),
            jax.ShapeDtypeStruct((rows, 128), F32),
        ],
        scratch_shapes=[pltpu.VMEM((2 * heads, width), BF16)],
        compiler_params=params,
        name="gate",
    )(y, z_proj, c_conv, reach_two, enter)

    total = jnp.sum(squares, axis=-1, keepdims=True)
    count = lax.axis_size("tp")
    own = total
    for k in range(1, count):
        total = total + lax.ppermute(own, "tp", [(i, (i + k) % count) for i in range(count)])
    part = rows // 2
    return pl.pallas_call(
        functools.partial(norm_kernel, channels=inner * count),
        grid=(2,),
        in_specs=[
            pl.BlockSpec((part, inner), lambda r: (r, 0)),
            full(rows, 1),
            full(1, inner),
        ],
        out_specs=pl.BlockSpec((part, inner), lambda r: (r, 0)),
        out_shape=jax.ShapeDtypeStruct((rows, inner), BF16),
        compiler_params=params,
        name="norm",
    )(gated, total, norm_gain.reshape(1, inner))


def solution(mesh):
    in_specs = (
        P("seq", "tp"),
        P("seq", None, "tp"),
        P("seq", "tp"),
        P("seq", "tp"),
        P(None, "tp"),
        P(None, None, "tp"),
        P("tp"),
        P(None, "tp"),
        P("tp"),
        P("tp"),
        P("tp"),
        P("tp"),
        P("seq"),
    )
    return jax.shard_map(
        on_device, mesh=mesh, in_specs=in_specs, out_specs=P("seq", "tp"), check_vma=False
    )
```
